256 devices in a mesh: lon: 32 (over y_hi, z, core), lat: 8 (over x, y_lo).
Axes of the slice: x: 4, y: 4 (y_hi: 2, y_lo: 2; y = y_hi * 2 + y_lo), z: 8, core: 2. Of those that a mesh axis runs over, the one named last changes fastest.
Arguments:
- previous: float32 [2, 2, 1024, 8192], P(None, None, 'lon', 'lat'), may hold values from -6 to 6
- current: float32 [2, 2, 1024, 8192], P(None, None, 'lon', 'lat'), may hold values from -6 to 6
- east_speed: float32 [2, 1024, 8192], P(None, 'lon', 'lat'), may hold values from -0.28 to 0.28, as said below
- north_speed: float32 [2, 1024, 8192], P(None, 'lon', 'lat'), may hold values from -0.28 to 0.28, as said below
- east_mix: float32 [2, 1024, 8192], P(None, 'lon', 'lat'), may hold values from 0 to 0.1, as said below
- north_mix: float32 [2, 1024, 8192], P(None, 'lon', 'lat'), may hold values from 0 to 0.1, as said below
- sea_mask: int32 [1024, 8192], P('lon', 'lat'), may hold values from 0 to 1, as said below
Outputs:
- lagged: float32 [2, 2, 1024, 8192], P(None, None, 'lon', 'lat')
- latest: float32 [2, 2, 1024, 8192], P(None, None, 'lon', 'lat')
The draws below stay inside these ranges and needn't reach their ends.
Inputs may be any that keep to these rules, and one draw needn't show every extreme that they name: `sea_mask`: the land cells form rectangular blocks of 32 x 1024 cells, coastal blocks with scattered land and open ocean with a few islands; which block is which is random. `east_speed`: zero on every face that touches a land cell; the east face of the last longitude joins it to the first. `north_speed`: zero on every face that touches a land cell and on the whole top latitude. `east_mix`: zero on every face that touches a land cell. `north_mix`: zero on every face that touches a land cell; on the top latitude the face across the fold joins cell i to cell 1024 - 1 - i and the value at i equals that at 1023 - i.
All inputs are finite; a program needn't handle non-finite values.
Results may differ from the reference program's by a relative error of at most 0.00002.
Values sent between devices are 32-bit elements; how exact they have to be, the bound alone decides.
A program may use at most 64 MiB of HBM per device.

```python
import jax
import jax.numpy as jnp
from jax import lax

CX = 32
CY = 1024
STEPS = 6
NX = 1024
NY = 8192


def ocean_layout(key):
    block_kind = jax.random.randint(jax.random.fold_in(key, 101), (NX // CX, NY // CY), 0, 4)
    kind_cells = jnp.repeat(jnp.repeat(block_kind, CX, axis=0), CY, axis=1)
    speckle = jax.random.randint(jax.random.fold_in(key, 102), (NX, NY), 0, 16)
    coastal = jnp.where(speckle < 8, 1, 0)
    openwater = jnp.where(speckle < 15, 1, 0)
    return jnp.where(kind_cells == 0, 0, jnp.where(kind_cells == 1, coastal, openwater)).astype(jnp.int32)


def face_masks(key):
    sea_float = ocean_layout(key).astype(jnp.float32)
    east_face = sea_float * jnp.roll(sea_float, -1, axis=0)
    north_face = sea_float * jnp.concatenate([sea_float[:, 1:], jnp.zeros((NX, 1), jnp.float32)], axis=1)
    fold_face = sea_float[:, NY - 1] * sea_float[::-1, NY - 1]
    return (east_face, north_face, fold_face)


def draw_sea_mask(key, part):
    return ocean_layout(key)


def draw_east_speed(key, part):
    east_face, north_face, fold_face = face_masks(key)
    key = jax.random.fold_in(key, 11)
    values = jax.random.uniform(key, (2, NX, NY), jnp.float32, -0.28, 0.28)
    return (values * east_face[None]).astype(jnp.float32)


def draw_north_speed(key, part):
    east_face, north_face, fold_face = face_masks(key)
    key = jax.random.fold_in(key, 12)
    values = jax.random.uniform(key, (2, NX, NY), jnp.float32, -0.28, 0.28)
    return (values * north_face[None]).astype(jnp.float32)


def draw_east_mix(key, part):
    east_face, north_face, fold_face = face_masks(key)
    key = jax.random.fold_in(key, 13)
    values = jnp.exp(jax.random.uniform(key, (2, NX, NY), jnp.float32, jnp.log(0.01), jnp.log(0.1)))
    return (values * east_face[None]).astype(jnp.float32)


def draw_north_mix(key, part):
    east_face, north_face, fold_face = face_masks(key)
    key = jax.random.fold_in(key, 14)
    values = jnp.exp(jax.random.uniform(key, (2, NX, NY), jnp.float32, jnp.log(0.01), jnp.log(0.1)))
    top_row = 0.5 * (values[:, :, NY - 1] + values[:, ::-1, NY - 1]) * fold_face[None]
    inner = values[:, :, :NY - 1] * north_face[None, :, :NY - 1]
    return jnp.concatenate([inner, top_row[:, :, None]], axis=2).astype(jnp.float32)


def shard_levels(key, extent, split, low, top_value):
    factor_of, own = 1.0, jax.random.fold_in(key, 6)
    for position, parts in split:
        heights = jnp.exp(jax.random.uniform(jax.random.fold_in(own, position), (parts,), jnp.float32, low / len(split), top_value / len(split)))
        factor_of = factor_of * jnp.repeat(heights, extent[position] // parts).reshape([-1 if axis == position else 1 for axis in range(len(extent))])
    return factor_of


def scatter_about(key, shape, deviation, most, shards=(), dtype=jnp.bfloat16):
    drawn = deviation * jax.random.normal(key, shape, jnp.float32)
    if shards:
        drawn = drawn * shard_levels(key, shape, shards, -0.22, 0.18)
    return jnp.clip(drawn, -most, most).astype(dtype)


def setup_inputs(seed: int = 0) -> dict:
    key_of = jax.random.split(jax.random.key(seed), 8)
    return {
        "previous": scatter_about(key_of[0], (2, 2, NX, NY), 1.0, 6.0, ((2, 32), (3, 8)), jnp.float32),
        "current": scatter_about(key_of[1], (2, 2, NX, NY), 1.0, 6.0, ((2, 32), (3, 8)), jnp.float32),
        "east_speed": draw_east_speed(jax.random.fold_in(key_of[7], 71), 0),
        "north_speed": draw_north_speed(jax.random.fold_in(key_of[7], 71), 0),
        "east_mix": draw_east_mix(jax.random.fold_in(key_of[7], 71), 0),
        "north_mix": draw_north_mix(jax.random.fold_in(key_of[7], 71), 0),
        "sea_mask": draw_sea_mask(jax.random.fold_in(key_of[7], 71), 0),
    }


GAMMA = 0.1


def leapfrog(older, newer, east_flow, north_flow, east_diff, north_diff):
    width = newer.shape[1]
    height = newer.shape[2]
    wide_newer = jnp.concatenate([newer[:, width - 2:], newer, newer[:, :2]], axis=1)
    wide_older = jnp.concatenate([older[:, width - 2:], older, older[:, :2]], axis=1)
    flow_x = jnp.concatenate([east_flow[:, width - 1:], east_flow], axis=1)
    diff_x = jnp.concatenate([east_diff[:, width - 1:], east_diff], axis=1)
    far_west = wide_newer[:, 0:width + 1]
    near_west = wide_newer[:, 1:width + 2]
    near_east = wide_newer[:, 2:width + 3]
    far_east = wide_newer[:, 3:width + 4]
    east_flux = flow_x * (7.0 * (near_west + near_east) - (far_west + far_east)) / 12.0 - diff_x * (wide_older[:, 2:width + 3] - wide_older[:, 1:width + 2])
    east_div = east_flux[:, 1:] - east_flux[:, :-1]
    zero_rows = jnp.zeros((2, width, 2), jnp.float32)
    ghost_newer = jnp.flip(newer[:, :, height - 2:height], axis=(1, 2))
    ghost_older = jnp.flip(older[:, :, height - 2:height], axis=(1, 2))
    tall_newer = jnp.concatenate([zero_rows, newer, ghost_newer], axis=2)
    tall_older = jnp.concatenate([zero_rows, older, ghost_older], axis=2)
    zero_row = jnp.zeros((2, width, 1), jnp.float32)
    flow_y = jnp.concatenate([zero_row, north_flow], axis=2)
    diff_y = jnp.concatenate([zero_row, north_diff], axis=2)
    north_flux = flow_y * (7.0 * (tall_newer[..., 1:height + 2] + tall_newer[..., 2:height + 3]) - (tall_newer[..., 0:height + 1] + tall_newer[..., 3:height + 4])) / 12.0 - diff_y * (tall_older[..., 2:height + 3] - tall_older[..., 1:height + 2])
    north_div = north_flux[..., 1:] - north_flux[..., :-1]
    fresh_level = older - 2.0 * (east_div + north_div)
    filtered = newer + GAMMA * (older - 2.0 * newer + fresh_level)
    return filtered, fresh_level


def reference(previous, current, east_speed, north_speed, east_mix, north_mix, sea_mask):
    wet_cells = sea_mask.astype(jnp.float32)

    def one_tracer(pair_levels):
        older = pair_levels[0] * wet_cells
        newer = pair_levels[1] * wet_cells
        for step_index in range(STEPS):
            older, newer = leapfrog(older, newer, east_speed, north_speed, east_mix, north_mix)
        return jnp.stack([older, newer])

    result = lax.map(one_tracer, jnp.stack([previous, current], axis=1))
    return result[:, 0], result[:, 1]
```

```python
import functools

import jax
import jax.numpy as jnp
from jax import lax
from jax.experimental import pallas as pl
from jax.experimental.pallas import tpu as pltpu
from jax.sharding import PartitionSpec as P

STEPS = 6
GAMMA = 0.1
MESH = pl.DeviceIdType.MESH

LANES = 128
PAD = 16
HALO = 2 * STEPS
SLOT = 16
UNIT = HALO
ES, EM, NS, NM = 0, 2, 4, 6


def kernel(sizes, *refs):
    n_lon, n_lat, columns, height = sizes
    (prev_h, cur_h, es_h, ns_h, em_h, nm_h, mask_h, lag_h, lat_h) = refs[:9]
    (prev_v, cur_v, es_v, ns_v, em_v, nm_v, mask_v, state, coef, flux, pack, land) = refs[9:21]
    (in_sem, out_sem, lon_send, lon_recv, lat_send, lat_recv, self_sem) = refs[21:]
    tiles = height // LANES
    ring = tiles + 1
    row_tiles = columns // 8
    own = pl.ds(PAD, columns)

    lon, lat = lax.axis_index("lon"), lax.axis_index("lat")
    east, west = lax.rem(lon + 1, n_lon), lax.rem(lon + n_lon - 1, n_lon)
    is_top, is_bottom = lat == n_lat - 1, lat == 0
    north, south = jnp.minimum(lat + 1, n_lat - 1), jnp.maximum(lat - 1, 0)
    up_main = jnp.where(is_top, n_lon - 1 - lon, lon)
    up_east = jnp.where(is_top, lax.rem(n_lon - lon, n_lon), east)
    up_west = jnp.where(is_top, lax.rem(2 * n_lon - 2 - lon, n_lon), west)
    self_east = jnp.logical_and(is_top, up_east == lon)
    self_west = jnp.logical_and(is_top, up_west == lon)
    not_self_east = jnp.logical_not(self_east)
    not_self_west = jnp.logical_not(self_west)
    not_bottom = jnp.logical_not(is_bottom)

    staged = [
        (mask_h, mask_v), (cur_h, cur_v), (prev_h, prev_v),
        (es_h, es_v), (em_h, em_v), (ns_h, ns_v), (nm_h, nm_v),
    ]
    loads = [pltpu.make_async_copy(a, b, in_sem.at[i]) for i, (a, b) in enumerate(staged)]

    barrier = pltpu.get_barrier_semaphore()

    def greet(to_lon, to_lat):
        pl.semaphore_signal(
            barrier, inc=1, device_id={"lon": to_lon, "lat": to_lat}, device_id_type=MESH
        )

    greet(east, lat)
    greet(west, lat)
    greet(up_main, north)

    @pl.when(not_self_east)
    def _():
        greet(up_east, north)

    @pl.when(not_self_west)
    def _():
        greet(up_west, north)

    @pl.when(not_bottom)
    def _():
        greet(lon, south)
        greet(east, south)
        greet(west, south)

    for c in loads:
        c.start()

    for c in loads[:3]:
        c.wait()

    @pl.loop(0, tiles)
    def _(t):
        lanes = pl.ds(pl.multiple_of(t * LANES, LANES), LANES)
        for r in range(row_tiles):
            rows = slice(8 * r, 8 * r + 8)
            wet = mask_v[rows, lanes].astype(jnp.float32)
            for tr in range(2):
                for lv in range(2):
                    state[0, 1, tr, lv, t, PAD + 8 * r : PAD + 8 * r + 8, :] = (
                        cur_v[tr, lv, rows, lanes] * wet
                    )
                    state[0, 0, tr, lv, t, PAD + 8 * r : PAD + 8 * r + 8, :] = (
                        prev_v[tr, lv, rows, lanes] * wet
                    )

    for c in loads[3:]:
        c.wait()

    @pl.loop(0, tiles)
    def _(t):
        lanes = pl.ds(pl.multiple_of(t * LANES, LANES), LANES)
        for r in range(row_tiles):
            rows = slice(8 * r, 8 * r + 8)
            for field, ref, scale in (
                (ES, es_v, 2.0 / 12.0), (EM, em_v, 2.0), (NS, ns_v, 2.0 / 12.0), (NM, nm_v, 2.0),
            ):
                for lv in range(2):
                    coef[field + lv, t, PAD + 8 * r : PAD + 8 * r + 8, :] = (
                        ref[lv, rows, lanes] * scale
                    )

    lane = lax.broadcasted_iota(jnp.int32, (8, LANES), 1)
    sub = lax.broadcasted_iota(jnp.int32, (8, LANES), 0)
    slot_of_lane = lane // SLOT

    def field_rows(f, t, rows):
        if f < 8:
            return state[0, f // 4, (f // 2) % 2, f % 2, t, rows, :]
        return coef[f - 8, t, rows, :]

    top = jnp.where(is_top, 1, 0)
    turn = jnp.where(is_top, -1.0, 1.0)
    for r in range(row_tiles):
        rows = slice(PAD + 8 * r, PAD + 8 * r + 8)
        for h in range(2):
            up = jnp.zeros((8, LANES), jnp.float32)
            down = jnp.zeros((8, LANES), jnp.float32)
            for s in range(8):
                f = 8 * h + s
                here = slot_of_lane == s
                mine = field_rows(f, tiles - 1, rows)
                shift = (SLOT * s + SLOT) % LANES
                if f >= 8 + NS:
                    mine = pltpu.roll(mine, shift + top, 1)
                elif shift:
                    mine = pltpu.roll(mine, shift, 1)
                if f - 8 in (ES, ES + 1, NS, NS + 1):
                    mine = mine * turn
                up = jnp.where(here, mine, up)
                mine = field_rows(f, 0, rows)
                if s:
                    mine = pltpu.roll(mine, SLOT * s, 1)
                down = jnp.where(here, mine, down)
            pack[0, h, 8 * r : 8 * r + 8, :] = up
            pack[1, h, 8 * r : 8 * r + 8, :] = down

    @pl.when(is_top)
    def _():
        for h in range(2):
            turned = []
            for r in range(row_tiles):
                x = pack[0, h, 8 * r : 8 * r + 8, :]
                for bit in (1, 2, 4, 8):
                    x = jnp.where(
                        (lane & bit) == 0,
                        pltpu.roll(x, LANES - bit, 1),
                        pltpu.roll(x, bit, 1),
                    )
                for bit in (1, 2, 4):
                    x = jnp.where(
                        (sub & bit) == 0, pltpu.roll(x, 8 - bit, 0), pltpu.roll(x, bit, 0)
                    )
                turned.append(x)
            for r in range(row_tiles):
                pack[0, h, 8 * r : 8 * r + 8, :] = turned[row_tiles - 1 - r]

    @pl.when(is_bottom)
    def _():
        land[0] = jnp.zeros(land.shape[1:], jnp.float32)

    peers = 8 - jnp.where(is_bottom, 3, 0) - jnp.where(self_east, 1, 0) - jnp.where(self_west, 1, 0)
    pl.semaphore_wait(barrier, peers)

    own_rows = pl.ds(0, columns)
    last_rows, first_rows = pl.ds(columns - HALO, HALO), pl.ds(0, HALO)
    west_rows, east_rows = pl.ds(PAD - HALO, HALO), pl.ds(PAD + columns, HALO)

    def lat_copy(out, src_rows, side, dst_rows, slot, to_lon, to_lat):
        return pltpu.make_async_remote_copy(
            src_ref=pack.at[out, :, src_rows, :],
            dst_ref=land.at[side, :, dst_rows, :],
            send_sem=lat_send.at[out, slot],
            recv_sem=lat_recv.at[side, slot],
            device_id={"lon": to_lon, "lat": to_lat},
            device_id_type=MESH,
        )

    up_main_copy = lat_copy(0, own_rows, top, own, 0, up_main, north)
    up_east_copy = lat_copy(0, last_rows, top, west_rows, 1, up_east, north)
    up_west_copy = lat_copy(0, first_rows, top, east_rows, 2, up_west, north)
    down_copies = [
        lat_copy(1, own_rows, 1, own, 0, lon, south),
        lat_copy(1, last_rows, 1, west_rows, 1, east, south),
        lat_copy(1, first_rows, 1, east_rows, 2, west, south),
    ]
    self_east_copy = pltpu.make_async_copy(
        pack.at[0, :, last_rows, :], land.at[1, :, west_rows, :], self_sem.at[0]
    )
    self_west_copy = pltpu.make_async_copy(
        pack.at[0, :, first_rows, :], land.at[1, :, east_rows, :], self_sem.at[1]
    )

    up_main_copy.start()

    @pl.when(not_self_east)
    def _():
        up_east_copy.start()

    @pl.when(not_self_west)
    def _():
        up_west_copy.start()

    @pl.when(self_east)
    def _():
        self_east_copy.start()

    @pl.when(self_west)
    def _():
        self_west_copy.start()

    @pl.when(not_bottom)
    def _():
        for c in down_copies:
            c.start()

    def lon_copies(way, to_lon):
        newer, older, faces, cells = HALO, HALO - 1, HALO - 1, HALO - 2
        if way == 1:
            faces = cells

        def part(ref, width):
            if way == 0:
                src, dst = PAD + columns - width, PAD - width
            else:
                src, dst = PAD, PAD + columns
            return ref.at[..., pl.ds(src, width), :], ref.at[..., pl.ds(dst, width), :]

        parts = [
            part(state.at[0, 1, :, :, pl.ds(0, tiles)], newer),
            part(state.at[0, 0, :, :, pl.ds(0, tiles)], older),
            part(coef.at[pl.ds(ES, 4), pl.ds(0, tiles)], faces),
            part(coef.at[pl.ds(NS, 4), pl.ds(0, tiles)], cells),
        ]
        return [
            pltpu.make_async_remote_copy(
                src_ref=src,
                dst_ref=dst,
                send_sem=lon_send.at[way, i],
                recv_sem=lon_recv.at[way, i],
                device_id={"lon": to_lon, "lat": lat},
                device_id_type=MESH,
            )
            for i, (src, dst) in enumerate(parts)
        ]

    eastward, westward = lon_copies(0, east), lon_copies(1, west)
    for a, b in zip(eastward, westward):
        a.start()
        b.start()

    first_lane, last_lane = lane == 0, lane == LANES - 1

    def unit(k, r0, outs):
        wide = [(outs[0] - 1) % ring] + list(outs)
        beyond = (outs[-1] + 1) % ring

        @pl.loop(0, 2)
        def _(lv):
            for tr in range(2):
                older = state.at[k - 1, 0, tr, lv]
                newer = state.at[k - 1, 1, tr, lv]
                older_next = state.at[k, 0, tr, lv]
                newer_next = state.at[k, 1, tr, lv]
                es, em = coef.at[ES + lv], coef.at[EM + lv]
                ns, nm = coef.at[NS + lv], coef.at[NM + lv]

                def east_flux(t, r):
                    def q(ref, d):
                        return ref[t, pl.ds(r + d, 8), :]

                    near = q(newer, 0) + q(newer, 1)
                    far = q(newer, -1) + q(newer, 2)
                    return q(es, 0) * (7.0 * near - far) - q(em, 0) * (q(older, 1) - q(older, 0))

                low = {}
                high = {}
                for t in outs:
                    low[t] = east_flux(t, r0 - 1)
                    high[t] = east_flux(t, r0 + 4)
                    flux[t, 0:8, :] = low[t]
                    flux[t, 5:13, :] = high[t]

                for window in range(2):
                    r = r0 + 4 * window
                    rows = pl.ds(r, 8)

                    n, o, s = {}, {}, {}
                    for t in wide + [beyond]:
                        n[t] = newer[t, rows, :]
                    back = {t: pltpu.roll(n[t], LANES - 1, 1) for t in n}
                    for t in wide:
                        n1 = jnp.where(last_lane, back[(t + 1) % ring], back[t])
                        s[t] = n[t] + n1
                    s_end = n[beyond] + back[beyond]
                    s_back = {t: pltpu.roll(s[t], LANES - 1, 1) for t in wide}
                    s_back_end = pltpu.roll(s_end, LANES - 1, 1)
                    s_forth = {t: pltpu.roll(s[t], 1, 1) for t in wide}
                    for t in wide + [beyond]:
                        o[t] = older[t, rows, :]
                    o_back = {t: pltpu.roll(o[t], LANES - 1, 1) for t in o}
                    flow = {}
                    for i, t in enumerate(wide):
                        after = s_back[wide[i + 1]] if i + 1 < len(wide) else s_back_end
                        ahead = jnp.where(last_lane, after, s_back[t])
                        behind = s_forth[t]
                        if i > 0:
                            behind = jnp.where(first_lane, s_forth[wide[i - 1]], behind)
                        grad = jnp.where(last_lane, o_back[(t + 1) % ring], o_back[t]) - o[t]
                        flow[t] = (
                            ns[t, rows, :] * (8.0 * s[t] - (ahead + behind)) - nm[t, rows, :] * grad
                        )
                    flow_forth = {t: pltpu.roll(flow[t], 1, 1) for t in wide}
                    for i, t in enumerate(outs):
                        north_div = flow[t] - jnp.where(
                            first_lane, flow_forth[wide[i]], flow_forth[t]
                        )
                        if window == 0:
                            east_div = flux[t, 1:9, :] - low[t]
                        else:
                            east_div = high[t] - flux[t, 4:12, :]
                        fresh = o[t] - (east_div + north_div)
                        newer_next[t, rows, :] = fresh
                        older_next[t, rows, :] = (1.0 - 2.0 * GAMMA) * n[t] + GAMMA * (o[t] + fresh)

    def inner_place(u):
        k = jnp.where(u < 3, 1, jnp.where(u > 9, 6, (u - 3) // 2 + 2))
        j = jnp.where(u < 3, u, jnp.where(u < 9, lax.rem(u - 3, 2), 0))
        gap = jnp.where(u < 3, 8, 20 - 4 * k)
        return k, PAD + jnp.minimum(2 * k, 10) + j * gap

    @pl.loop(0, 11)
    def _(u):
        k, r0 = inner_place(u)
        unit(k, r0, list(range(tiles)))

    lat_in_south = [
        lat_copy(0, own_rows, 0, own, 0, lon, lat),
        lat_copy(0, last_rows, 0, west_rows, 1, lon, lat),
        lat_copy(0, first_rows, 0, east_rows, 2, lon, lat),
    ]

    @pl.when(not_bottom)
    def _():
        for c in lat_in_south:
            c.wait_recv()

    down_copies[0].wait_recv()

    @pl.when(not_self_east)
    def _():
        down_copies[1].wait_recv()

    @pl.when(not_self_west)
    def _():
        down_copies[2].wait_recv()

    @pl.when(self_east)
    def _():
        self_east_copy.wait()

    @pl.when(self_west)
    def _():
        self_west_copy.wait()

    for r in range((columns + 2 * PAD) // 8 - 1):
        begin = PAD - HALO + 8 * r
        rows = slice(begin, begin + 8)
        for f in range(16):
            h, s = divmod(f, 8)
            if f in (8 + ES, 9 + ES, 8 + EM, 9 + EM):
                north_part = land[1, h, pl.ds(begin + top, 8), :]
            else:
                north_part = land[1, h, rows, :]
            if s:
                north_part = pltpu.roll(north_part, LANES - SLOT * s, 1)
            south_part = land[0, h, rows, :]
            if s < 7:
                south_part = pltpu.roll(south_part, LANES - SLOT - SLOT * s, 1)
            both = jnp.where(lane < SLOT, north_part, south_part)
            if f < 8:
                state[0, f // 4, (f // 2) % 2, f % 2, tiles, rows, :] = both
            else:
                coef[f - 8, tiles, rows, :] = both

    @pl.loop(0, 11)
    def _(u):
        k, r0 = inner_place(u)
        unit(k, r0, [tiles - 1, tiles, 0])

    even = lax.rem(lon, 2) == 0

    def wait_west():
        for c in eastward:
            c.wait_recv()

    def wait_east():
        for c in westward:
            c.wait_recv()

    @pl.loop(0, 12)
    def _(u):
        late = u >= 6
        k = lax.rem(u, 6) + 1
        do_east = even != late

        @pl.when(jnp.logical_and(lax.rem(u, 6) == 0, do_east))
        def _():
            wait_east()

        @pl.when(jnp.logical_and(lax.rem(u, 6) == 0, jnp.logical_not(do_east)))
        def _():
            wait_west()

        r0 = jnp.where(do_east, PAD + columns - 2 * k, PAD + 2 * k - UNIT)
        unit(k, r0, list(range(ring)))

    stores = []
    for kind, ref in ((0, lag_h), (1, lat_h)):
        for t in range(tiles):
            c = pltpu.make_async_copy(
                state.at[STEPS, kind, :, :, t, own, :],
                ref.at[:, :, :, pl.ds(t * LANES, LANES)],
                out_sem.at[kind, t],
            )
            c.start()
            stores.append(c)

    for a, b in zip(eastward, westward):
        a.wait_send()
        b.wait_send()
    up_main_copy.wait_send()

    @pl.when(not_self_east)
    def _():
        up_east_copy.wait_send()

    @pl.when(not_self_west)
    def _():
        up_west_copy.wait_send()

    @pl.when(not_bottom)
    def _():
        for c in down_copies:
            c.wait_send()

    for c in stores:
        c.wait()


def solution(mesh):
    n_lon, n_lat = mesh.shape["lon"], mesh.shape["lat"]

    def shards(previous, current, east_speed, north_speed, east_mix, north_mix, sea_mask):
        columns, height = previous.shape[2:]
        tiles = height // LANES
        rows = columns + 2 * PAD
        field = jax.ShapeDtypeStruct(previous.shape, jnp.float32)
        f32 = jnp.float32
        return pl.pallas_call(
            functools.partial(kernel, (n_lon, n_lat, columns, height)),
            out_shape=(field, field),
            in_specs=[pl.BlockSpec(memory_space=pl.ANY)] * 7,
            out_specs=[pl.BlockSpec(memory_space=pl.ANY)] * 2,
            scratch_shapes=[
                pltpu.VMEM(previous.shape, f32),
                pltpu.VMEM(current.shape, f32),
                pltpu.VMEM(east_speed.shape, f32),
                pltpu.VMEM(north_speed.shape, f32),
                pltpu.VMEM(east_mix.shape, f32),
                pltpu.VMEM(north_mix.shape, f32),
                pltpu.VMEM(sea_mask.shape, sea_mask.dtype),
                pltpu.VMEM((STEPS + 1, 2, 2, 2, tiles + 1, rows, LANES), f32),
                pltpu.VMEM((8, tiles + 1, rows, LANES), f32),
                pltpu.VMEM((tiles + 1, 16, LANES), f32),
                pltpu.VMEM((2, 2, columns, LANES), f32),
                pltpu.VMEM((2, 2, rows, LANES), f32),
                pltpu.SemaphoreType.DMA((7,)),
                pltpu.SemaphoreType.DMA((2, tiles)),
                pltpu.SemaphoreType.DMA((2, 4)),
                pltpu.SemaphoreType.DMA((2, 4)),
                pltpu.SemaphoreType.DMA((2, 3)),
                pltpu.SemaphoreType.DMA((2, 3)),
                pltpu.SemaphoreType.DMA((2,)),
            ],
            compiler_params=pltpu.CompilerParams(
                collective_id=0, has_side_effects=True, vmem_limit_bytes=48 * 2**20
            ),
            cost_estimate=pl.CostEstimate(
                flops=30 * STEPS * previous.size, bytes_accessed=16 * previous.size, transcendentals=0
            ),
        )(previous, current, east_speed, north_speed, east_mix, north_mix, sea_mask)

    return jax.shard_map(
        shards,
        mesh=mesh,
        in_specs=(
            P(None, None, "lon", "lat"),
            P(None, None, "lon", "lat"),
            P(None, "lon", "lat"),
            P(None, "lon", "lat"),
            P(None, "lon", "lat"),
            P(None, "lon", "lat"),
            P("lon", "lat"),
        ),
        out_specs=(P(None, None, "lon", "lat"), P(None, None, "lon", "lat")),
        check_vma=False,
    )
```

```python
import functools

import jax
import jax.numpy as jnp
from jax import lax
from jax.experimental import pallas as pl
from jax.experimental.pallas import tpu as pltpu
from jax.sharding import PartitionSpec as P

STEPS = 6
GAMMA = 0.1
MESH = pl.DeviceIdType.MESH

LANES = 128
PAD = 16
HALO = 2 * STEPS
SLOT = 16
UNIT = HALO
ES, EM, NS, NM = 0, 2, 4, 6


def kernel(sizes, *refs):
    n_lon, n_lat, columns, height = sizes
    (prev_h, cur_h, es_h, ns_h, em_h, nm_h, mask_h, lag_h, lat_h) = refs[:9]
    (prev_v, cur_v, es_v, ns_v, em_v, nm_v, mask_v, state, coef, end_state, end_coef, flux, held, pack, land) = refs[9:24]
    (in_sem, out_sem, lon_send, lon_recv, lat_send, lat_recv, self_sem) = refs[24:]
    tiles = height // LANES
    ring = tiles + 1
    row_tiles = columns // 8
    own = pl.ds(PAD, columns)

    lon, lat = lax.axis_index("lon"), lax.axis_index("lat")
    east, west = lax.rem(lon + 1, n_lon), lax.rem(lon + n_lon - 1, n_lon)
    is_top, is_bottom = lat == n_lat - 1, lat == 0
    top = jnp.where(is_top, 1, 0)
    north, south = jnp.minimum(lat + 1, n_lat - 1), jnp.maximum(lat - 1, 0)
    up_main = jnp.where(is_top, n_lon - 1 - lon, lon)
    up_east = jnp.where(is_top, lax.rem(n_lon - lon, n_lon), east)
    up_west = jnp.where(is_top, lax.rem(2 * n_lon - 2 - lon, n_lon), west)
    self_east = jnp.logical_and(is_top, up_east == lon)
    self_west = jnp.logical_and(is_top, up_west == lon)
    not_self_east = jnp.logical_not(self_east)
    not_self_west = jnp.logical_not(self_west)
    not_bottom = jnp.logical_not(is_bottom)

    staged = [
        (mask_h, mask_v), (cur_h, cur_v), (prev_h, prev_v),
        (es_h, es_v), (em_h, em_v), (ns_h, ns_v), (nm_h, nm_v),
    ]
    loads = [pltpu.make_async_copy(a, b, in_sem.at[i]) for i, (a, b) in enumerate(staged)]

    barrier = pltpu.get_barrier_semaphore()

    def greet(to_lon, to_lat):
        pl.semaphore_signal(
            barrier, inc=1, device_id={"lon": to_lon, "lat": to_lat}, device_id_type=MESH
        )

    greet(east, lat)
    greet(west, lat)
    greet(up_main, north)

    @pl.when(not_self_east)
    def _():
        greet(up_east, north)

    @pl.when(not_self_west)
    def _():
        greet(up_west, north)

    @pl.when(not_bottom)
    def _():
        greet(lon, south)
        greet(east, south)
        greet(west, south)

    for c in loads:
        c.start()

    lane = lax.broadcasted_iota(jnp.int32, (8, LANES), 1)
    sub = lax.broadcasted_iota(jnp.int32, (8, LANES), 0)

    def roll(x, shift):
        return pltpu.roll(x, shift % LANES, 1)

    def exchange(tile):
        for bit in (1, 2, 4):
            keep = (lane & bit) == 0
            new = list(tile)
            for t in range(tiles):
                if not t & bit:
                    x, y = tile[t], tile[t + bit]
                    new[t] = jnp.where(keep, x, roll(y, bit))
                    new[t + bit] = jnp.where(keep, roll(x, -bit), y)
            tile = new
        return tile

    def lay_out(pieces):
        for load, target, ends, r in pieces:
            tile = [load(slice(8 * r, 8 * r + 8), slice(t * LANES, (t + 1) * LANES)) for t in range(tiles)]
            rows = slice(PAD + 8 * r, PAD + 8 * r + 8)
            both = jnp.where(lane < LANES // 2, roll(tile[0], HALO), roll(tile[-1], -HALO))
            target[tiles, rows, :] = both
            ends[8 * r : 8 * r + 8, :] = both
            for t, x in enumerate(exchange(tile)):
                target[t, rows, :] = x

    def masked(ref, tr, lv):
        return lambda rows, lanes: ref[tr, lv, rows, lanes] * mask_v[rows, lanes].astype(jnp.float32)

    def scaled(ref, lv, scale):
        return lambda rows, lanes: ref[lv, rows, lanes] * scale

    def level(kind, ref):
        lay_out([
            (masked(ref, tr, lv), state.at[0, kind, tr, lv], end_state.at[kind, tr, lv], r)
            for tr in range(2) for lv in range(2) for r in range(row_tiles)
        ])

    def coefs(*fields):
        lay_out([
            (scaled(ref, lv, scale), coef.at[field + lv], end_coef.at[field + lv], r)
            for field, ref, scale in fields for lv in range(2) for r in range(row_tiles)
        ])

    loads[0].wait()
    loads[1].wait()
    level(1, cur_v)
    loads[2].wait()
    level(0, prev_v)

    def lon_copies(way, to_lon):
        newer, older, faces, cells = HALO, HALO - 1, HALO - 1, HALO - 2
        if way == 1:
            faces = cells

        def part(ref, ends, width):
            begin = columns - width if way == 0 else 0
            dst = pl.ds(PAD - width if way == 0 else PAD + columns, width)
            return [
                (ref.at[..., pl.ds(0, tiles), pl.ds(PAD + begin, width), :], ref.at[..., pl.ds(0, tiles), dst, :]),
                (ends.at[..., pl.ds(begin, width), :], ref.at[..., tiles, dst, :]),
            ]

        parts = (
            part(state.at[0, 1], end_state.at[1], newer)
            + part(state.at[0, 0], end_state.at[0], older)
            + part(coef.at[pl.ds(ES, 4)], end_coef.at[pl.ds(ES, 4)], faces)
            + part(coef.at[pl.ds(NS, 4)], end_coef.at[pl.ds(NS, 4)], cells)
        )
        return [
            pltpu.make_async_remote_copy(
                src_ref=src,
                dst_ref=dst,
                send_sem=lon_send.at[way, i],
                recv_sem=lon_recv.at[way, i],
                device_id={"lon": to_lon, "lat": lat},
                device_id_type=MESH,
            )
            for i, (src, dst) in enumerate(parts)
        ]

    eastward, westward = lon_copies(0, east), lon_copies(1, west)
    peers = 8 - jnp.where(is_bottom, 3, 0) - jnp.where(self_east, 1, 0) - jnp.where(self_west, 1, 0)
    pl.semaphore_wait(barrier, peers)

    def send(first, last):
        for i in range(first, last):
            eastward[i].start()
            westward[i].start()

    send(0, 4)
    loads[3].wait()
    loads[4].wait()
    coefs((ES, es_v, 2.0 / 12.0), (EM, em_v, 2.0))
    send(4, 6)
    loads[5].wait()
    loads[6].wait()
    coefs((NS, ns_v, 2.0 / 12.0), (NM, nm_v, 2.0))
    send(6, 8)

    slot_of_lane = lane // SLOT

    def field_rows(f, rows):
        if f < 8:
            return end_state[f // 4, (f // 2) % 2, f % 2, rows, :]
        return end_coef[f - 8, rows, :]

    turn = jnp.where(is_top, -1.0, 1.0)
    for r in range(row_tiles):
        rows = slice(8 * r, 8 * r + 8)
        for h in range(2):
            up = jnp.zeros((8, LANES), jnp.float32)
            down = jnp.zeros((8, LANES), jnp.float32)
            for s in range(8):
                f = 8 * h + s
                here = slot_of_lane == s
                mine = field_rows(f, rows)
                shift = (SLOT * s - (LANES - HALO - SLOT)) % LANES
                if f >= 8 + NS:
                    high = pltpu.roll(mine, shift + top, 1)
                else:
                    high = roll(mine, shift)
                if f - 8 in (ES, ES + 1, NS, NS + 1):
                    high = high * turn
                up = jnp.where(here, high, up)
                down = jnp.where(here, roll(mine, SLOT * s - HALO), down)
            pack[0, h, 8 * r : 8 * r + 8, :] = up
            pack[1, h, 8 * r : 8 * r + 8, :] = down

    @pl.when(is_top)
    def _():
        for h in range(2):
            turned = []
            for r in range(row_tiles):
                x = pack[0, h, 8 * r : 8 * r + 8, :]
                for bit in (1, 2, 4, 8):
                    x = jnp.where(
                        (lane & bit) == 0,
                        pltpu.roll(x, LANES - bit, 1),
                        pltpu.roll(x, bit, 1),
                    )
                for bit in (1, 2, 4):
                    x = jnp.where(
                        (sub & bit) == 0, pltpu.roll(x, 8 - bit, 0), pltpu.roll(x, bit, 0)
                    )
                turned.append(x)
            for r in range(row_tiles):
                pack[0, h, 8 * r : 8 * r + 8, :] = turned[row_tiles - 1 - r]

    @pl.when(is_bottom)
    def _():
        land[0] = jnp.zeros(land.shape[1:], jnp.float32)

    own_rows = pl.ds(0, columns)
    last_rows, first_rows = pl.ds(columns - HALO, HALO), pl.ds(0, HALO)
    west_rows, east_rows = pl.ds(PAD - HALO, HALO), pl.ds(PAD + columns, HALO)

    def lat_copy(out, src_rows, side, dst_rows, slot, to_lon, to_lat):
        return pltpu.make_async_remote_copy(
            src_ref=pack.at[out, :, src_rows, :],
            dst_ref=land.at[side, :, dst_rows, :],
            send_sem=lat_send.at[out, slot],
            recv_sem=lat_recv.at[side, slot],
            device_id={"lon": to_lon, "lat": to_lat},
            device_id_type=MESH,
        )

    up_main_copy = lat_copy(0, own_rows, top, own, 0, up_main, north)
    up_east_copy = lat_copy(0, last_rows, top, west_rows, 1, up_east, north)
    up_west_copy = lat_copy(0, first_rows, top, east_rows, 2, up_west, north)
    down_copies = [
        lat_copy(1, own_rows, 1, own, 0, lon, south),
        lat_copy(1, last_rows, 1, west_rows, 1, east, south),
        lat_copy(1, first_rows, 1, east_rows, 2, west, south),
    ]
    self_east_copy = pltpu.make_async_copy(
        pack.at[0, :, last_rows, :], land.at[1, :, west_rows, :], self_sem.at[0]
    )
    self_west_copy = pltpu.make_async_copy(
        pack.at[0, :, first_rows, :], land.at[1, :, east_rows, :], self_sem.at[1]
    )

    up_main_copy.start()

    @pl.when(not_self_east)
    def _():
        up_east_copy.start()

    @pl.when(not_self_west)
    def _():
        up_west_copy.start()

    @pl.when(self_east)
    def _():
        self_east_copy.start()

    @pl.when(self_west)
    def _():
        self_west_copy.start()

    @pl.when(not_bottom)
    def _():
        for c in down_copies:
            c.start()

    def up(x):
        return jnp.where(lane >= LANES - 8, roll(x, -9), roll(x, -8))

    def down(x):
        return jnp.where(lane < 8, roll(x, 9), roll(x, 8))

    def after(x):
        return [roll(x[0], -1)] if len(x) == 1 else x[1:] + [up(x[0])]

    def before(x):
        return [roll(x[0], 1)] if len(x) == 1 else [down(x[-1])] + x[:-1]

    def advance(old, lv, r0, group):
        for t in group:
            es = [coef[ES + lv, t, pl.ds(r0 + d, 8), :] for d in (-1, 4)]
            em = [coef[EM + lv, t, pl.ds(r0 + d, 8), :] for d in (-1, 4)]
            for tr in range(2):
                for i, d in enumerate((-1, 4)):

                    def q(kind, by):
                        return old[kind, tr, lv, t, pl.ds(r0 + d + by, 8), :]

                    near, far = q(1, 0) + q(1, 1), q(1, -1) + q(1, 2)
                    flux[lv, tr, t, 5 * i : 5 * i + 8, :] = es[i] * (7.0 * near - far) - em[i] * (
                        q(0, 1) - q(0, 0)
                    )
        for w in range(2):
            rows = pl.ds(r0 + 4 * w, 8)
            ns = [coef[NS + lv, t, rows, :] for t in group]
            nm = [coef[NM + lv, t, rows, :] for t in group]
            for tr in range(2):
                n = [old[1, tr, lv, t, rows, :] for t in group]
                o = [old[0, tr, lv, t, rows, :] for t in group]
                s = [a + b for a, b in zip(n, after(n))]
                flow = [
                    u * (8.0 * here - (a + b)) - v * (o1 - o0)
                    for u, v, here, a, b, o1, o0 in zip(ns, nm, s, after(s), before(s), after(o), o)
                ]
                for i, (t, f, f0) in enumerate(zip(group, flow, before(flow))):
                    east_div = (
                        flux[lv, tr, t, 4 * w + 1 : 4 * w + 9, :] - flux[lv, tr, t, 4 * w : 4 * w + 8, :]
                    )
                    fresh = o[i] - (east_div + (f - f0))
                    held[lv, 1, tr, w, t] = fresh
                    held[lv, 0, tr, w, t] = (1.0 - 2.0 * GAMMA) * n[i] + GAMMA * (o[i] + fresh)

    def unit(k, r0, groups):
        old, new = state.at[k - 1], state.at[k]
        for lv in range(2):
            for group in groups:
                advance(old, lv, r0, group)
        for lv in range(2):
            for w in range(2):
                for tr in range(2):
                    for t in sum(groups, []):
                        for kind in range(2):
                            new[kind, tr, lv, t, pl.ds(r0 + 4 * w, 8), :] = held[lv, kind, tr, w, t]

    main, edge = list(range(tiles)), [tiles]

    def inner_place(u):
        k = jnp.where(u < 3, 1, jnp.where(u > 9, 6, (u - 3) // 2 + 2))
        j = jnp.where(u < 3, u, jnp.where(u < 9, lax.rem(u - 3, 2), 0))
        gap = jnp.where(u < 3, 8, 20 - 4 * k)
        return k, PAD + jnp.minimum(2 * k, 10) + j * gap

    @pl.loop(0, 11)
    def _(u):
        k, r0 = inner_place(u)
        unit(k, r0, [main])

    lat_in_south = [
        lat_copy(0, own_rows, 0, own, 0, lon, lat),
        lat_copy(0, last_rows, 0, west_rows, 1, lon, lat),
        lat_copy(0, first_rows, 0, east_rows, 2, lon, lat),
    ]

    @pl.when(not_bottom)
    def _():
        for c in lat_in_south:
            c.wait_recv()

    down_copies[0].wait_recv()

    @pl.when(not_self_east)
    def _():
        down_copies[1].wait_recv()

    @pl.when(not_self_west)
    def _():
        down_copies[2].wait_recv()

    @pl.when(self_east)
    def _():
        self_east_copy.wait()

    @pl.when(self_west)
    def _():
        self_west_copy.wait()

    def unpack(begins):
        done = []
        for begin in begins:
            rows = pl.ds(begin, 8)
            for f in range(16):
                h, s = divmod(f, 8)
                source = rows
                if f in (8 + ES, 9 + ES, 8 + EM, 9 + EM):
                    source = pl.ds(begin + top, 8)
                north_part = roll(land[1, h, source, :], LANES - HALO - SLOT * s)
                south_part = roll(land[0, h, rows, :], HALO - SLOT - SLOT * s)
                if f < 8:
                    target = state.at[0, f // 4, (f // 2) % 2, f % 2, tiles]
                else:
                    target = coef.at[f - 8, tiles]
                inside = jnp.where(lane < HALO, south_part, target[rows, :])
                done.append((target, rows, jnp.where(lane >= LANES - HALO, north_part, inside)))
        for target, rows, value in done:
            target[rows, :] = value

    unpack([PAD + 8 * r for r in range(row_tiles)])

    @pl.loop(0, 11)
    def _(u):
        k, r0 = inner_place(u)
        unit(k, r0, [edge])

    even = lax.rem(lon, 2) == 0

    def finish(first_row, slot):
        for r in range(2):
            rows = pl.ds(pl.multiple_of(first_row + 8 * r, 8), 8)
            source = pl.ds(pl.multiple_of(PAD + first_row + 8 * r, 8), 8)
            for kind, target in ((0, prev_v), (1, cur_v)):
                for tr in range(2):
                    for lv in range(2):
                        tile = exchange([state[STEPS, kind, tr, lv, t, source, :] for t in main])
                        ends = state[STEPS, kind, tr, lv, tiles, source, :]
                        tile[0] = jnp.where(lane < HALO, roll(ends, -HALO), tile[0])
                        tile[-1] = jnp.where(lane >= LANES - HALO, roll(ends, HALO), tile[-1])
                        for t in main:
                            target[tr, lv, rows, t * LANES : (t + 1) * LANES] = tile[t]
        rows = pl.ds(pl.multiple_of(first_row, 16), 16)
        copies = [
            pltpu.make_async_copy(
                source.at[:, :, rows, :], target.at[:, :, rows, :], out_sem.at[slot, i]
            )
            for i, (source, target) in enumerate(((prev_v, lag_h), (cur_v, lat_h)))
        ]
        for c in copies:
            c.start()
        return copies

    @pl.loop(0, 2)
    def _(late):
        do_east = even != (late == 1)

        @pl.when(do_east)
        def _():
            for c in westward:
                c.wait_recv()

        @pl.when(jnp.logical_not(do_east))
        def _():
            for c in eastward:
                c.wait_recv()

        side = jnp.where(do_east, PAD + columns, PAD - HALO)
        unpack([side, side + 4])

        @pl.loop(1, STEPS + 1)
        def _(k):
            unit(k, jnp.where(do_east, PAD + columns - 2 * k, PAD + 2 * k - UNIT), [main, edge])

        finish(jnp.where(do_east, columns // 2, 0), late)

    finished = [
        pltpu.make_async_copy(
            source.at[:, :, pl.ds(0, 16), :], target.at[:, :, pl.ds(0, 16), :], out_sem.at[slot, i]
        )
        for slot in range(2)
        for i, (source, target) in enumerate(((prev_v, lag_h), (cur_v, lat_h)))
    ]

    for a, b in zip(eastward, westward):
        a.wait_send()
        b.wait_send()
    up_main_copy.wait_send()

    @pl.when(not_self_east)
    def _():
        up_east_copy.wait_send()

    @pl.when(not_self_west)
    def _():
        up_west_copy.wait_send()

    @pl.when(not_bottom)
    def _():
        for c in down_copies:
            c.wait_send()

    for c in finished:
        c.wait()


def solution(mesh):
    n_lon, n_lat = mesh.shape["lon"], mesh.shape["lat"]

    def shards(previous, current, east_speed, north_speed, east_mix, north_mix, sea_mask):
        columns, height = previous.shape[2:]
        tiles = height // LANES
        rows = columns + 2 * PAD
        field = jax.ShapeDtypeStruct(previous.shape, jnp.float32)
        f32 = jnp.float32
        return pl.pallas_call(
            functools.partial(kernel, (n_lon, n_lat, columns, height)),
            out_shape=(field, field),
            in_specs=[pl.BlockSpec(memory_space=pl.ANY)] * 7,
            out_specs=[pl.BlockSpec(memory_space=pl.ANY)] * 2,
            scratch_shapes=[
                pltpu.VMEM(previous.shape, f32),
                pltpu.VMEM(current.shape, f32),
                pltpu.VMEM(east_speed.shape, f32),
                pltpu.VMEM(north_speed.shape, f32),
                pltpu.VMEM(east_mix.shape, f32),
                pltpu.VMEM(north_mix.shape, f32),
                pltpu.VMEM(sea_mask.shape, sea_mask.dtype),
                pltpu.VMEM((STEPS + 1, 2, 2, 2, tiles + 1, rows, LANES), f32),
                pltpu.VMEM((8, tiles + 1, rows, LANES), f32),
                pltpu.VMEM((2, 2, 2, columns, LANES), f32),
                pltpu.VMEM((8, columns, LANES), f32),
                pltpu.VMEM((2, 2, tiles + 1, 16, LANES), f32),
                pltpu.VMEM((2, 2, 2, 2, tiles + 1, 8, LANES), f32),
                pltpu.VMEM((2, 2, columns, LANES), f32),
                pltpu.VMEM((2, 2, rows, LANES), f32),
                pltpu.SemaphoreType.DMA((7,)),
                pltpu.SemaphoreType.DMA((2, 2)),
                pltpu.SemaphoreType.DMA((2, 8)),
                pltpu.SemaphoreType.DMA((2, 8)),
                pltpu.SemaphoreType.DMA((2, 3)),
                pltpu.SemaphoreType.DMA((2, 3)),
                pltpu.SemaphoreType.DMA((2,)),
            ],
            compiler_params=pltpu.CompilerParams(
                collective_id=0, has_side_effects=True, vmem_limit_bytes=60 * 2**20
            ),
            cost_estimate=pl.CostEstimate(
                flops=30 * STEPS * previous.size, bytes_accessed=16 * previous.size, transcendentals=0
            ),
        )(previous, current, east_speed, north_speed, east_mix, north_mix, sea_mask)

    return jax.shard_map(
        shards,
        mesh=mesh,
        in_specs=(
            P(None, None, "lon", "lat"),
            P(None, None, "lon", "lat"),
            P(None, "lon", "lat"),
            P(None, "lon", "lat"),
            P(None, "lon", "lat"),
            P(None, "lon", "lat"),
            P("lon", "lat"),
        ),
        out_specs=(P(None, None, "lon", "lat"), P(None, None, "lon", "lat")),
        check_vma=False,
    )
```

```python
import functools

import jax
import jax.numpy as jnp
from jax import lax
from jax.experimental import pallas as pl
from jax.experimental.pallas import tpu as pltpu
from jax.sharding import PartitionSpec as P

STEPS = 6
GAMMA = 0.1
MESH = pl.DeviceIdType.MESH

LANES = 128
PAD = 16
HALO = 2 * STEPS
SLOT = 16
UNIT = HALO
OLD, NEW = 0, 1
ES, EM, NS, NM = range(4)
SCALES = (2.0 / 12.0, 2.0, 2.0 / 12.0, 2.0)


def kernel(sizes, *refs):
    n_lon, n_lat, columns, height = sizes
    (prev_h, cur_h, es_h, ns_h, em_h, nm_h, mask_h, lag_h, lat_h) = refs[:9]
    (mask_v, state_v, coef_v, state, coef, ends, div, held, pack, land) = refs[9:19]
    (in_sem, out_sem, lon_send, lon_recv, lat_send, lat_recv, self_sem) = refs[19:]
    tiles = height // LANES
    ring = tiles + 1
    row_tiles = columns // 8
    own = pl.ds(PAD, columns)

    lon, lat = lax.axis_index("lon"), lax.axis_index("lat")
    east, west = lax.rem(lon + 1, n_lon), lax.rem(lon + n_lon - 1, n_lon)
    is_top, is_bottom = lat == n_lat - 1, lat == 0
    top = jnp.where(is_top, 1, 0)
    north, south = jnp.minimum(lat + 1, n_lat - 1), jnp.maximum(lat - 1, 0)
    up_main = jnp.where(is_top, n_lon - 1 - lon, lon)
    up_east = jnp.where(is_top, lax.rem(n_lon - lon, n_lon), east)
    up_west = jnp.where(is_top, lax.rem(2 * n_lon - 2 - lon, n_lon), west)
    self_east = jnp.logical_and(is_top, up_east == lon)
    self_west = jnp.logical_and(is_top, up_west == lon)
    not_self_east = jnp.logical_not(self_east)
    not_self_west = jnp.logical_not(self_west)
    not_bottom = jnp.logical_not(is_bottom)

    staged = [(mask_h, mask_v), (cur_h, state_v.at[NEW]), (prev_h, state_v.at[OLD])] + [
        (ref, coef_v.at[field]) for field, ref in enumerate((es_h, em_h, ns_h, nm_h))
    ]
    loads = [pltpu.make_async_copy(a, b, in_sem.at[i]) for i, (a, b) in enumerate(staged)]

    barrier = pltpu.get_barrier_semaphore()

    def greet(to_lon, to_lat):
        pl.semaphore_signal(
            barrier, inc=1, device_id={"lon": to_lon, "lat": to_lat}, device_id_type=MESH
        )

    greet(east, lat)
    greet(west, lat)
    greet(up_main, north)

    @pl.when(not_self_east)
    def _():
        greet(up_east, north)

    @pl.when(not_self_west)
    def _():
        greet(up_west, north)

    @pl.when(not_bottom)
    def _():
        greet(lon, south)
        greet(east, south)
        greet(west, south)

    for c in loads:
        c.start()

    lane = lax.broadcasted_iota(jnp.int32, (8, LANES), 1)
    sub = lax.broadcasted_iota(jnp.int32, (8, LANES), 0)

    def roll(x, shift):
        return pltpu.roll(x, shift % LANES, 1)

    def exchange(tile):
        for bit in (1, 2, 4):
            keep = (lane & bit) == 0
            new = list(tile)
            for t in range(tiles):
                if not t & bit:
                    x, y = tile[t], tile[t + bit]
                    new[t] = jnp.where(keep, x, roll(y, bit))
                    new[t + bit] = jnp.where(keep, roll(x, -bit), y)
            tile = new
        return tile

    def lay_out(tile, target, end, r):
        rows = slice(PAD + 8 * r, PAD + 8 * r + 8)
        both = jnp.where(lane < LANES // 2, roll(tile[0], HALO), roll(tile[-1], -HALO))
        target[tiles, rows, :] = both
        end[8 * r : 8 * r + 8, :] = both
        for t, x in enumerate(exchange(tile)):
            target[t, rows, :] = x

    def block(r, t):
        return slice(8 * r, 8 * r + 8), slice(t * LANES, (t + 1) * LANES)

    for c in loads[:3]:
        c.wait()

    @pl.loop(0, 2)
    def _(lv):
        for r in range(row_tiles):
            wet = [mask_v[block(r, t)].astype(jnp.float32) for t in range(tiles)]
            for kind in (OLD, NEW):
                for tr in range(2):
                    lay_out(
                        [state_v[kind, tr, lv, *block(r, t)] * wet[t] for t in range(tiles)],
                        state.at[0, lv, kind, tr],
                        ends.at[lv, 2 * kind + tr],
                        r,
                    )

    for c in loads[3:]:
        c.wait()

    @pl.loop(0, 2)
    def _(lv):
        for field in range(4):
            for r in range(row_tiles):
                lay_out(
                    [coef_v[field, lv, *block(r, t)] * SCALES[field] for t in range(tiles)],
                    coef.at[lv, field],
                    ends.at[lv, 4 + field],
                    r,
                )

    slot_of_lane = lane // SLOT
    turn = jnp.where(is_top, -1.0, 1.0)

    @pl.loop(0, 2)
    def _(lv):
        for r in range(row_tiles):
            rows = slice(8 * r, 8 * r + 8)
            up = jnp.zeros((8, LANES), jnp.float32)
            down = jnp.zeros((8, LANES), jnp.float32)
            for s in range(8):
                here = slot_of_lane == s
                mine = ends[lv, s, rows, :]
                shift = (SLOT * s - (LANES - HALO - SLOT)) % LANES
                high = pltpu.roll(mine, shift + top, 1) if s in (4 + NS, 4 + NM) else roll(mine, shift)
                if s in (4 + ES, 4 + NS):
                    high = high * turn
                up = jnp.where(here, high, up)
                down = jnp.where(here, roll(mine, SLOT * s - HALO), down)
            pack[0, lv, rows, :] = up
            pack[1, lv, rows, :] = down

    @pl.when(is_top)
    def _():
        for h in range(2):
            turned = []
            for r in range(row_tiles):
                x = pack[0, h, 8 * r : 8 * r + 8, :]
                for bit in (1, 2, 4, 8):
                    x = jnp.where(
                        (lane & bit) == 0,
                        pltpu.roll(x, LANES - bit, 1),
                        pltpu.roll(x, bit, 1),
                    )
                for bit in (1, 2, 4):
                    x = jnp.where(
                        (sub & bit) == 0, pltpu.roll(x, 8 - bit, 0), pltpu.roll(x, bit, 0)
                    )
                turned.append(x)
            for r in range(row_tiles):
                pack[0, h, 8 * r : 8 * r + 8, :] = turned[row_tiles - 1 - r]

    @pl.when(is_bottom)
    def _():
        land[0] = jnp.zeros(land.shape[1:], jnp.float32)

    peers = 8 - jnp.where(is_bottom, 3, 0) - jnp.where(self_east, 1, 0) - jnp.where(self_west, 1, 0)
    pl.semaphore_wait(barrier, peers)

    own_rows = pl.ds(0, columns)
    last_rows, first_rows = pl.ds(columns - HALO, HALO), pl.ds(0, HALO)
    west_rows, east_rows = pl.ds(PAD - HALO, HALO), pl.ds(PAD + columns, HALO)

    def lat_copy(out, src_rows, side, dst_rows, slot, to_lon, to_lat):
        return pltpu.make_async_remote_copy(
            src_ref=pack.at[out, :, src_rows, :],
            dst_ref=land.at[side, :, dst_rows, :],
            send_sem=lat_send.at[out, slot],
            recv_sem=lat_recv.at[side, slot],
            device_id={"lon": to_lon, "lat": to_lat},
            device_id_type=MESH,
        )

    up_main_copy = lat_copy(0, own_rows, top, own, 0, up_main, north)
    up_east_copy = lat_copy(0, last_rows, top, west_rows, 1, up_east, north)
    up_west_copy = lat_copy(0, first_rows, top, east_rows, 2, up_west, north)
    down_copies = [
        lat_copy(1, own_rows, 1, own, 0, lon, south),
        lat_copy(1, last_rows, 1, west_rows, 1, east, south),
        lat_copy(1, first_rows, 1, east_rows, 2, west, south),
    ]
    self_east_copy = pltpu.make_async_copy(
        pack.at[0, :, last_rows, :], land.at[1, :, west_rows, :], self_sem.at[0]
    )
    self_west_copy = pltpu.make_async_copy(
        pack.at[0, :, first_rows, :], land.at[1, :, east_rows, :], self_sem.at[1]
    )

    up_main_copy.start()

    @pl.when(not_self_east)
    def _():
        up_east_copy.start()

    @pl.when(not_self_west)
    def _():
        up_west_copy.start()

    @pl.when(self_east)
    def _():
        self_east_copy.start()

    @pl.when(self_west)
    def _():
        self_west_copy.start()

    @pl.when(not_bottom)
    def _():
        for c in down_copies:
            c.start()

    def lon_copies(way, lv, to_lon):
        def part(source, first, target, width):
            begin = first + (columns - width if way == 0 else 0)
            dst = PAD - width if way == 0 else PAD + columns
            return source.at[..., pl.ds(begin, width), :], target.at[..., pl.ds(dst, width), :]

        main_tiles = pl.ds(0, tiles)
        new, old = state.at[0, lv, NEW, :, main_tiles], state.at[0, lv, OLD, :, main_tiles]
        east_coef = coef.at[lv, pl.ds(ES, 2), main_tiles]
        north_coef = coef.at[lv, pl.ds(NS, 2), main_tiles]
        parts = [
            part(new, PAD, new, HALO),
            part(old, PAD, old, HALO - 1),
            part(east_coef, PAD, east_coef, HALO - 1 if way == 0 else HALO - 2),
            part(north_coef, PAD, north_coef, HALO - 2),
            part(ends.at[lv, pl.ds(0, 2)], 0, state.at[0, lv, OLD, :, tiles], HALO),
            part(ends.at[lv, pl.ds(2, 2)], 0, state.at[0, lv, NEW, :, tiles], HALO),
            part(ends.at[lv, pl.ds(4, 4)], 0, coef.at[lv, :, tiles], HALO),
        ]
        return [
            pltpu.make_async_remote_copy(
                src_ref=src,
                dst_ref=dst,
                send_sem=lon_send.at[way, lv, i],
                recv_sem=lon_recv.at[way, lv, i],
                device_id={"lon": to_lon, "lat": lat},
                device_id_type=MESH,
            )
            for i, (src, dst) in enumerate(parts)
        ]

    eastward = [lon_copies(0, lv, east) for lv in range(2)]
    westward = [lon_copies(1, lv, west) for lv in range(2)]
    for lv in range(2):
        for a, b in zip(eastward[lv], westward[lv]):
            a.start()
            b.start()

    def up(x):
        return jnp.where(lane >= LANES - 8, roll(x, -9), roll(x, -8))

    def down(x):
        return jnp.where(lane < 8, roll(x, 9), roll(x, 8))

    def after(x):
        return [roll(x[0], -1)] if len(x) == 1 else x[1:] + [up(x[0])]

    def before(x):
        return [roll(x[0], 1)] if len(x) == 1 else [down(x[-1])] + x[:-1]

    def eastern(x):
        y = [pltpu.roll(a, 7, 0) for a in x]
        return [jnp.where(sub == 7, b, a) for a, b in zip(y, y[1:])] + y[-1:]

    def western(x):
        y = [pltpu.roll(a, 1, 0) for a in x]
        return y[:1] + [jnp.where(sub == 0, a, b) for a, b in zip(y, y[1:])]

    def advance(k, lv, slot, base, count, group):
        frames = [pl.ds(base + 8 * i, 8) for i in range(count)]
        old = state.at[k - 1, lv]
        for t in group:
            es = [coef[lv, ES, t, rows, :] for rows in frames]
            em = [coef[lv, EM, t, rows, :] for rows in frames]
            for tr in range(2):
                n = [old[NEW, tr, t, rows, :] for rows in frames]
                o = [old[OLD, tr, t, rows, :] for rows in frames]
                near = [a + b for a, b in zip(n, eastern(n))]
                flow = [
                    u * (8.0 * here - (a + b)) - v * (o1 - o0)
                    for u, v, here, a, b, o1, o0 in zip(
                        es, em, near, eastern(near), western(near), eastern(o), o
                    )
                ]
                for i, (a, b) in enumerate(zip(flow, western(flow))):
                    div[slot, tr, t, 8 * i : 8 * i + 8, :] = a - b
        for i, rows in enumerate(frames):
            mine = slice(8 * i, 8 * i + 8)
            for tr in range(2):
                n = [old[NEW, tr, t, rows, :] for t in group]
                o = [old[OLD, tr, t, rows, :] for t in group]
                near = [a + b for a, b in zip(n, after(n))]
                flow = [
                    coef[lv, NS, t, rows, :] * (8.0 * here - (a + b)) - coef[lv, NM, t, rows, :] * (o1 - o0)
                    for t, here, a, b, o1, o0 in zip(
                        group, near, after(near), before(near), after(o), o
                    )
                ]
                for j, (t, a, b) in enumerate(zip(group, flow, before(flow))):
                    fresh = o[j] - (div[slot, tr, t, mine, :] + (a - b))
                    held[slot, NEW, tr, t, mine, :] = fresh
                    held[slot, OLD, tr, t, mine, :] = (1.0 - 2.0 * GAMMA) * n[j] + GAMMA * (
                        o[j] + fresh
                    )

    def keep(k, lv, slot, base, windows, group):
        for kind in (NEW, OLD):
            for tr in range(2):
                for t in group:
                    for w in windows:
                        state[k, lv, kind, tr, t, pl.ds(base + w, 8), :] = held[
                            slot, kind, tr, t, w : w + 8, :
                        ]

    main, edge = list(range(tiles)), [tiles]

    def inner_place(u):
        k = jnp.where(u < 3, 1, jnp.where(u > 9, 6, (u - 3) // 2 + 2))
        j = jnp.where(u < 3, u, jnp.where(u < 9, lax.rem(u - 3, 2), 0))
        gap = jnp.where(u < 3, 8, 20 - 4 * k)
        return k, PAD + jnp.minimum(2 * k, 10) + j * gap

    @pl.loop(0, 11)
    def _(u):
        k, r0 = inner_place(u)
        for lv in range(2):
            advance(k, lv, lv, r0 - 2, 2, main)
        for lv in range(2):
            keep(k, lv, lv, r0 - 2, (2, 6), main)

    lat_in_south = [
        lat_copy(0, own_rows, 0, own, 0, lon, lat),
        lat_copy(0, last_rows, 0, west_rows, 1, lon, lat),
        lat_copy(0, first_rows, 0, east_rows, 2, lon, lat),
    ]

    @pl.when(not_bottom)
    def _():
        for c in lat_in_south:
            c.wait_recv()

    down_copies[0].wait_recv()

    @pl.when(not_self_east)
    def _():
        down_copies[1].wait_recv()

    @pl.when(not_self_west)
    def _():
        down_copies[2].wait_recv()

    @pl.when(self_east)
    def _():
        self_east_copy.wait()

    @pl.when(self_west)
    def _():
        self_west_copy.wait()

    def unpack(lv, begins):
        done = []
        for begin in begins:
            rows = pl.ds(begin, 8)
            for f in range(8):
                source = pl.ds(begin + top, 8) if f in (4 + ES, 4 + EM) else rows
                north_part = roll(land[1, lv, source, :], LANES - HALO - SLOT * f)
                south_part = roll(land[0, lv, rows, :], HALO - SLOT - SLOT * f)
                if f < 4:
                    target = state.at[0, lv, f // 2, f % 2, tiles]
                else:
                    target = coef.at[lv, f - 4, tiles]
                inside = jnp.where(lane < HALO, south_part, target[rows, :])
                done.append((target, rows, jnp.where(lane >= LANES - HALO, north_part, inside)))
        for target, rows, value in done:
            target[rows, :] = value

    @pl.loop(0, 2)
    def _(lv):
        unpack(lv, [PAD + 8 * r for r in range(row_tiles)])

    @pl.loop(1, STEPS + 1)
    def _(k):
        for lv in range(2):
            advance(k, lv, lv, PAD, row_tiles, edge)
        for lv in range(2):
            keep(k, lv, lv, PAD, range(0, columns, 8), edge)

    even = lax.rem(lon, 2) == 0

    def output_copy(kind, lv, rows, slot):
        return pltpu.make_async_copy(
            state_v.at[kind, :, lv, rows, :],
            (lag_h, lat_h)[kind].at[:, lv, rows, :],
            out_sem.at[slot, kind],
        )

    @pl.loop(0, 4)
    def _(turn_no):
        lv = lax.rem(turn_no, 2)
        do_east = even != (turn_no >= 2)

        @pl.when(do_east)
        def _():
            for c in lon_copies(1, lv, west):
                c.wait_recv()

        @pl.when(jnp.logical_not(do_east))
        def _():
            for c in lon_copies(0, lv, east):
                c.wait_recv()

        side = jnp.where(do_east, PAD + columns, PAD - HALO)
        unpack(lv, [side, side + 4])

        @pl.loop(1, STEPS + 1)
        def _(k):
            base = jnp.where(do_east, PAD + columns - 2 * k, PAD + 2 * k - UNIT) - 2
            for group in (main, edge):
                advance(k, lv, 0, base, 2, group)
            for group in (main, edge):
                keep(k, lv, 0, base, (2, 6), group)

        first = pl.multiple_of(jnp.where(do_east, columns // 2, 0), 16)
        for r in range(2):
            rows = pl.ds(pl.multiple_of(first + 8 * r, 8), 8)
            source = pl.ds(pl.multiple_of(PAD + first + 8 * r, 8), 8)
            for kind in (OLD, NEW):
                for tr in range(2):
                    tile = exchange([state[STEPS, lv, kind, tr, t, source, :] for t in main])
                    end = state[STEPS, lv, kind, tr, tiles, source, :]
                    tile[0] = jnp.where(lane < HALO, roll(end, -HALO), tile[0])
                    tile[-1] = jnp.where(lane >= LANES - HALO, roll(end, HALO), tile[-1])
                    for t in main:
                        state_v[kind, tr, lv, rows, t * LANES : (t + 1) * LANES] = tile[t]
        for kind in (OLD, NEW):
            output_copy(kind, lv, pl.ds(first, 16), turn_no).start()

    for c in sum(eastward + westward, []):
        c.wait_send()
    up_main_copy.wait_send()

    @pl.when(not_self_east)
    def _():
        up_east_copy.wait_send()

    @pl.when(not_self_west)
    def _():
        up_west_copy.wait_send()

    @pl.when(not_bottom)
    def _():
        for c in down_copies:
            c.wait_send()

    for slot in range(4):
        for kind in (OLD, NEW):
            output_copy(kind, 0, pl.ds(0, 16), slot).wait()


def solution(mesh):
    n_lon, n_lat = mesh.shape["lon"], mesh.shape["lat"]

    def shards(previous, current, east_speed, north_speed, east_mix, north_mix, sea_mask):
        columns, height = previous.shape[2:]
        tiles = height // LANES
        rows = columns + 2 * PAD
        field = jax.ShapeDtypeStruct(previous.shape, jnp.float32)
        f32 = jnp.float32
        return pl.pallas_call(
            functools.partial(kernel, (n_lon, n_lat, columns, height)),
            out_shape=(field, field),
            in_specs=[pl.BlockSpec(memory_space=pl.ANY)] * 7,
            out_specs=[pl.BlockSpec(memory_space=pl.ANY)] * 2,
            scratch_shapes=[
                pltpu.VMEM(sea_mask.shape, sea_mask.dtype),
                pltpu.VMEM((2, *previous.shape), f32),
                pltpu.VMEM((4, *east_speed.shape), f32),
                pltpu.VMEM((STEPS + 1, 2, 2, 2, tiles + 1, rows, LANES), f32),
                pltpu.VMEM((2, 4, tiles + 1, rows, LANES), f32),
                pltpu.VMEM((2, 8, columns, LANES), f32),
                pltpu.VMEM((2, 2, tiles + 1, columns, LANES), f32),
                pltpu.VMEM((2, 2, 2, tiles + 1, columns, LANES), f32),
                pltpu.VMEM((2, 2, columns, LANES), f32),
                pltpu.VMEM((2, 2, rows, LANES), f32),
                pltpu.SemaphoreType.DMA((7,)),
                pltpu.SemaphoreType.DMA((4, 2)),
                pltpu.SemaphoreType.DMA((2, 2, 7)),
                pltpu.SemaphoreType.DMA((2, 2, 7)),
                pltpu.SemaphoreType.DMA((2, 3)),
                pltpu.SemaphoreType.DMA((2, 3)),
                pltpu.SemaphoreType.DMA((2,)),
            ],
            compiler_params=pltpu.CompilerParams(
                collective_id=0, has_side_effects=True, vmem_limit_bytes=60 * 2**20
            ),
            cost_estimate=pl.CostEstimate(
                flops=30 * STEPS * previous.size, bytes_accessed=16 * previous.size, transcendentals=0
            ),
        )(previous, current, east_speed, north_speed, east_mix, north_mix, sea_mask)

    return jax.shard_map(
        shards,
        mesh=mesh,
        in_specs=(
            P(None, None, "lon", "lat"),
            P(None, None, "lon", "lat"),
            P(None, "lon", "lat"),
            P(None, "lon", "lat"),
            P(None, "lon", "lat"),
            P(None, "lon", "lat"),
            P("lon", "lat"),
        ),
        out_specs=(P(None, None, "lon", "lat"), P(None, None, "lon", "lat")),
        check_vma=False,
    )
```

```python
import functools

import jax
import jax.numpy as jnp
from jax import lax
from jax.experimental import pallas as pl
from jax.experimental.pallas import tpu as pltpu
from jax.sharding import PartitionSpec as P

STEPS = 6
GAMMA = 0.1
MESH = pl.DeviceIdType.MESH

LANES = 128
PAD = 16
HALO = 2 * STEPS
SLOT = 16
UNIT = HALO
OLD, NEW = 0, 1
ES, EM, NS, NM = range(4)
SCALES = (2.0 / 12.0, 2.0)


def kernel(sizes, *refs):
    n_lon, n_lat, columns, height = sizes
    (prev_h, cur_h, es_h, ns_h, em_h, nm_h, mask_h, lag_h, lat_h) = refs[:9]
    (mask_v, state_v, coef_v, state, coef, ends, div, held, pack, land) = refs[9:19]
    (in_sem, lon_send, lon_recv, lat_send, lat_recv, self_sem) = refs[19:]
    tiles = height // LANES
    ring = tiles + 1
    row_tiles = columns // 8
    own = pl.ds(PAD, columns)

    lon, lat = lax.axis_index("lon"), lax.axis_index("lat")
    east, west = lax.rem(lon + 1, n_lon), lax.rem(lon + n_lon - 1, n_lon)
    is_top, is_bottom = lat == n_lat - 1, lat == 0
    top = jnp.where(is_top, 1, 0)
    north, south = jnp.minimum(lat + 1, n_lat - 1), jnp.maximum(lat - 1, 0)
    up_main = jnp.where(is_top, n_lon - 1 - lon, lon)
    up_east = jnp.where(is_top, lax.rem(n_lon - lon, n_lon), east)
    up_west = jnp.where(is_top, lax.rem(2 * n_lon - 2 - lon, n_lon), west)
    self_east = jnp.logical_and(is_top, up_east == lon)
    self_west = jnp.logical_and(is_top, up_west == lon)
    not_self_east = jnp.logical_not(self_east)
    not_self_west = jnp.logical_not(self_west)
    not_bottom = jnp.logical_not(is_bottom)

    staged = [(mask_h, mask_v), (cur_h, state_v.at[NEW]), (prev_h, state_v.at[OLD])] + [
        (ref, coef_v.at[field]) for field, ref in enumerate((es_h, em_h, ns_h, nm_h))
    ]
    loads = [pltpu.make_async_copy(a, b, in_sem.at[i]) for i, (a, b) in enumerate(staged)]

    barrier = pltpu.get_barrier_semaphore()

    def greet(to_lon, to_lat):
        pl.semaphore_signal(
            barrier, inc=1, device_id={"lon": to_lon, "lat": to_lat}, device_id_type=MESH
        )

    greet(east, lat)
    greet(west, lat)
    greet(up_main, north)

    @pl.when(not_self_east)
    def _():
        greet(up_east, north)

    @pl.when(not_self_west)
    def _():
        greet(up_west, north)

    @pl.when(not_bottom)
    def _():
        greet(lon, south)
        greet(east, south)
        greet(west, south)

    for c in loads:
        c.start()

    lane = lax.broadcasted_iota(jnp.int32, (8, LANES), 1)
    sub = lax.broadcasted_iota(jnp.int32, (8, LANES), 0)

    def roll(x, shift):
        return pltpu.roll(x, shift % LANES, 1)

    def permute(x, source):
        return jnp.take_along_axis(x, source, axis=1)

    def exchange(tile):
        for bit in (1, 2, 4):
            keep = (lane & bit) == 0
            new = list(tile)
            for t in range(tiles):
                if not t & bit:
                    x, y = tile[t], tile[t + bit]
                    crossing = permute(jnp.where(keep, y, x), lane ^ bit)
                    new[t] = jnp.where(keep, x, crossing)
                    new[t + bit] = jnp.where(keep, crossing, y)
            tile = new
        return tile

    def lay_out(tile, target, end, r):
        rows = slice(PAD + 8 * r, PAD + 8 * r + 8)
        both = jnp.where(lane < LANES // 2, roll(tile[0], HALO), roll(tile[-1], -HALO))
        target[tiles, rows, :] = both
        end[8 * r : 8 * r + 8, :] = both
        for t, x in enumerate(exchange(tile)):
            target[t, rows, :] = x

    def block(r, t):
        return slice(8 * r, 8 * r + 8), slice(t * LANES, (t + 1) * LANES)

    for c in loads[:3]:
        c.wait()

    @pl.loop(0, 4)
    def _(i):
        lv, kind = i // 2, lax.rem(i, 2)
        for r in range(row_tiles):
            wet = [mask_v[block(r, t)].astype(jnp.float32) for t in range(tiles)]
            for tr in range(2):
                lay_out(
                    [state_v[kind, tr, lv, *block(r, t)] * wet[t] for t in range(tiles)],
                    state.at[0, lv, kind, tr],
                    ends.at[lv, 2 * kind + tr],
                    r,
                )

    for c in loads[3:]:
        c.wait()

    @pl.loop(0, 4)
    def _(i):
        lv, pair = i // 2, lax.rem(i, 2)
        for j in range(2):
            for r in range(row_tiles):
                lay_out(
                    [coef_v[2 * pair + j, lv, *block(r, t)] * SCALES[j] for t in range(tiles)],
                    coef.at[lv, 2 * pair + j],
                    ends.at[lv, 4 + 2 * pair + j],
                    r,
                )

    slot_of_lane = lane // SLOT
    turn = jnp.where(is_top, -1.0, 1.0)

    @pl.loop(0, 2)
    def _(lv):
        for r in range(row_tiles):
            rows = slice(8 * r, 8 * r + 8)
            up = jnp.zeros((8, LANES), jnp.float32)
            down = jnp.zeros((8, LANES), jnp.float32)
            for s in range(8):
                here = slot_of_lane == s
                mine = ends[lv, s, rows, :]
                shift = (SLOT * s - (LANES - HALO - SLOT)) % LANES
                high = pltpu.roll(mine, shift + top, 1) if s in (4 + NS, 4 + NM) else roll(mine, shift)
                if s in (4 + ES, 4 + NS):
                    high = high * turn
                up = jnp.where(here, high, up)
                down = jnp.where(here, roll(mine, SLOT * s - HALO), down)
            pack[0, lv, rows, :] = up
            pack[1, lv, rows, :] = down

    @pl.when(is_top)
    def _():
        for h in range(2):
            turned = []
            for r in range(row_tiles):
                x = pack[0, h, 8 * r : 8 * r + 8, :]
                x = permute(x, lane ^ (SLOT - 1))
                for bit in (1, 2, 4):
                    x = jnp.where(
                        (sub & bit) == 0, pltpu.roll(x, 8 - bit, 0), pltpu.roll(x, bit, 0)
                    )
                turned.append(x)
            for r in range(row_tiles):
                pack[0, h, 8 * r : 8 * r + 8, :] = turned[row_tiles - 1 - r]

    @pl.when(is_bottom)
    def _():
        land[0] = jnp.zeros(land.shape[1:], jnp.float32)

    peers = 8 - jnp.where(is_bottom, 3, 0) - jnp.where(self_east, 1, 0) - jnp.where(self_west, 1, 0)
    pl.semaphore_wait(barrier, peers)

    own_rows = pl.ds(0, columns)
    last_rows, first_rows = pl.ds(columns - HALO, HALO), pl.ds(0, HALO)
    west_rows, east_rows = pl.ds(PAD - HALO, HALO), pl.ds(PAD + columns, HALO)

    def lat_copy(out, src_rows, side, dst_rows, slot, to_lon, to_lat):
        return pltpu.make_async_remote_copy(
            src_ref=pack.at[out, :, src_rows, :],
            dst_ref=land.at[side, :, dst_rows, :],
            send_sem=lat_send.at[out, slot],
            recv_sem=lat_recv.at[side, slot],
            device_id={"lon": to_lon, "lat": to_lat},
            device_id_type=MESH,
        )

    up_main_copy = lat_copy(0, own_rows, top, own, 0, up_main, north)
    up_east_copy = lat_copy(0, last_rows, top, west_rows, 1, up_east, north)
    up_west_copy = lat_copy(0, first_rows, top, east_rows, 2, up_west, north)
    down_copies = [
        lat_copy(1, own_rows, 1, own, 0, lon, south),
        lat_copy(1, last_rows, 1, west_rows, 1, east, south),
        lat_copy(1, first_rows, 1, east_rows, 2, west, south),
    ]
    self_east_copy = pltpu.make_async_copy(
        pack.at[0, :, last_rows, :], land.at[1, :, west_rows, :], self_sem.at[0]
    )
    self_west_copy = pltpu.make_async_copy(
        pack.at[0, :, first_rows, :], land.at[1, :, east_rows, :], self_sem.at[1]
    )

    up_main_copy.start()

    @pl.when(not_self_east)
    def _():
        up_east_copy.start()

    @pl.when(not_self_west)
    def _():
        up_west_copy.start()

    @pl.when(self_east)
    def _():
        self_east_copy.start()

    @pl.when(self_west)
    def _():
        self_west_copy.start()

    @pl.when(not_bottom)
    def _():
        for c in down_copies:
            c.start()

    def lon_copies(way, lv, to_lon):
        def part(source, first, target, width):
            begin = first + (columns - width if way == 0 else 0)
            dst = PAD - width if way == 0 else PAD + columns
            return source.at[..., pl.ds(begin, width), :], target.at[..., pl.ds(dst, width), :]

        main_tiles = pl.ds(0, tiles)
        new, old = state.at[0, lv, NEW, :, main_tiles], state.at[0, lv, OLD, :, main_tiles]
        east_coef = coef.at[lv, pl.ds(ES, 2), main_tiles]
        north_coef = coef.at[lv, pl.ds(NS, 2), main_tiles]
        parts = [
            part(new, PAD, new, HALO),
            part(old, PAD, old, HALO - 1),
            part(east_coef, PAD, east_coef, HALO - 1 if way == 0 else HALO - 2),
            part(north_coef, PAD, north_coef, HALO - 2),
            part(ends.at[lv, pl.ds(0, 2)], 0, state.at[0, lv, OLD, :, tiles], HALO),
            part(ends.at[lv, pl.ds(2, 2)], 0, state.at[0, lv, NEW, :, tiles], HALO),
            part(ends.at[lv, pl.ds(4, 4)], 0, coef.at[lv, :, tiles], HALO),
        ]
        return [
            pltpu.make_async_remote_copy(
                src_ref=src,
                dst_ref=dst,
                send_sem=lon_send.at[way, lv, i],
                recv_sem=lon_recv.at[way, lv, i],
                device_id={"lon": to_lon, "lat": lat},
                device_id_type=MESH,
            )
            for i, (src, dst) in enumerate(parts)
        ]

    eastward = [lon_copies(0, lv, east) for lv in range(2)]
    westward = [lon_copies(1, lv, west) for lv in range(2)]
    for lv in range(2):
        for a, b in zip(eastward[lv], westward[lv]):
            a.start()
            b.start()

    next_lane = jnp.where(lane >= LANES - 8, lane - (LANES - 9), lane + 8)
    last_lane = jnp.where(lane < 8, lane + (LANES - 9), lane - 8)

    def after(x):
        return [roll(x[0], -1)] if len(x) == 1 else x[1:] + [permute(x[0], next_lane)]

    def before(x):
        return [roll(x[0], 1)] if len(x) == 1 else [permute(x[-1], last_lane)] + x[:-1]

    def eastern(x):
        y = [pltpu.roll(a, 7, 0) for a in x]
        return [jnp.where(sub == 7, b, a) for a, b in zip(y, y[1:])] + y[-1:]

    def western(x):
        y = [pltpu.roll(a, 1, 0) for a in x]
        return y[:1] + [jnp.where(sub == 0, a, b) for a, b in zip(y, y[1:])]

    def advance(k, lv, slot, base, count, group):
        frames = [pl.ds(base + 8 * i, 8) for i in range(count)]
        old = state.at[k - 1, lv]
        for t in group:
            es = [coef[lv, ES, t, rows, :] for rows in frames]
            em = [coef[lv, EM, t, rows, :] for rows in frames]
            for tr in range(2):
                n = [old[NEW, tr, t, rows, :] for rows in frames]
                o = [old[OLD, tr, t, rows, :] for rows in frames]
                near = [a + b for a, b in zip(n, eastern(n))]
                flow = [
                    u * (8.0 * here - (a + b)) - v * (o1 - o0)
                    for u, v, here, a, b, o1, o0 in zip(
                        es, em, near, eastern(near), western(near), eastern(o), o
                    )
                ]
                for i, (a, b) in enumerate(zip(flow, western(flow))):
                    div[slot, tr, t, 8 * i : 8 * i + 8, :] = a - b
        for i, rows in enumerate(frames):
            mine = slice(8 * i, 8 * i + 8)
            for tr in range(2):
                n = [old[NEW, tr, t, rows, :] for t in group]
                o = [old[OLD, tr, t, rows, :] for t in group]
                near = [a + b for a, b in zip(n, after(n))]
                flow = [
                    coef[lv, NS, t, rows, :] * (8.0 * here - (a + b)) - coef[lv, NM, t, rows, :] * (o1 - o0)
                    for t, here, a, b, o1, o0 in zip(
                        group, near, after(near), before(near), after(o), o
                    )
                ]
                for j, (t, a, b) in enumerate(zip(group, flow, before(flow))):
                    fresh = o[j] - (div[slot, tr, t, mine, :] + (a - b))
                    held[slot, NEW, tr, t, mine, :] = fresh
                    held[slot, OLD, tr, t, mine, :] = (1.0 - 2.0 * GAMMA) * n[j] + GAMMA * (
                        o[j] + fresh
                    )

    def keep(k, lv, slot, base, windows, group):
        for kind in (NEW, OLD):
            for tr in range(2):
                for t in group:
                    for w in windows:
                        state[k, lv, kind, tr, t, pl.ds(base + w, 8), :] = held[
                            slot, kind, tr, t, w : w + 8, :
                        ]

    main, edge = list(range(tiles)), [tiles]

    def inner_place(u):
        k = jnp.where(u < 3, 1, jnp.where(u > 9, 6, (u - 3) // 2 + 2))
        j = jnp.where(u < 3, u, jnp.where(u < 9, lax.rem(u - 3, 2), 0))
        gap = jnp.where(u < 3, 8, 20 - 4 * k)
        return k, PAD + jnp.minimum(2 * k, 10) + j * gap

    @pl.loop(0, 11)
    def _(u):
        k, r0 = inner_place(u)
        for lv in range(2):
            advance(k, lv, lv, r0 - 2, 2, main)
        for lv in range(2):
            keep(k, lv, lv, r0 - 2, (2, 6), main)

    even = lax.rem(lon, 2) == 0
    outs = (lag_h, lat_h)
    wide = range((columns + 2 * HALO) // 8)

    def side_in(do_east, lv):
        @pl.when(do_east)
        def _():
            for c in lon_copies(1, lv, west):
                c.wait_recv()

        @pl.when(jnp.logical_not(do_east))
        def _():
            for c in lon_copies(0, lv, east):
                c.wait_recv()

    def side_base(do_east, k):
        return jnp.where(do_east, PAD + columns - 2 * k, PAD + 2 * k - UNIT) - 2

    def finish(do_east, lv):
        first = pl.multiple_of(jnp.where(do_east, columns // 2, 0), 16)

        @pl.loop(0, 2)
        def _(kind_no):
            for r in range(2):
                rows = pl.ds(pl.multiple_of(first + 8 * r, 8), 8)
                source = pl.ds(pl.multiple_of(PAD + first + 8 * r, 8), 8)
                for tr in range(2):
                    tile = exchange([state[STEPS, lv, kind_no, tr, t, source, :] for t in main])
                    for t in main:
                        state_v[kind_no, tr, lv, rows, t * LANES : (t + 1) * LANES] = tile[t]

    @pl.loop(0, 2)
    def _(lv):
        side_in(even, lv)

        @pl.loop(1, STEPS + 1)
        def _(k):
            base = side_base(even, k)
            advance(k, lv, 0, base, 2, main)
            keep(k, lv, 0, base, (2, 6), main)

        finish(even, lv)

    lat_in_south = [
        lat_copy(0, own_rows, 0, own, 0, lon, lat),
        lat_copy(0, last_rows, 0, west_rows, 1, lon, lat),
        lat_copy(0, first_rows, 0, east_rows, 2, lon, lat),
    ]

    @pl.when(not_bottom)
    def _():
        for c in lat_in_south:
            c.wait_recv()

    down_copies[0].wait_recv()

    @pl.when(not_self_east)
    def _():
        down_copies[1].wait_recv()

    @pl.when(not_self_west)
    def _():
        down_copies[2].wait_recv()

    @pl.when(self_east)
    def _():
        self_east_copy.wait()

    @pl.when(self_west)
    def _():
        self_west_copy.wait()

    def unpack(lv, begins):
        done = []
        for begin in begins:
            rows = pl.ds(begin, 8)
            for f in range(8):
                source = pl.ds(begin + top, 8) if f in (4 + ES, 4 + EM) else rows
                north_part = roll(land[1, lv, source, :], LANES - HALO - SLOT * f)
                south_part = roll(land[0, lv, rows, :], HALO - SLOT - SLOT * f)
                if f < 4:
                    target = state.at[0, lv, f // 2, f % 2, tiles]
                else:
                    target = coef.at[lv, f - 4, tiles]
                inside = jnp.where(lane < HALO, south_part, target[rows, :])
                done.append((target, rows, jnp.where(lane >= LANES - HALO, north_part, inside)))
        for target, rows, value in done:
            target[rows, :] = value

    @pl.loop(0, 2)
    def _(lv):
        do_east = jnp.logical_not(even)
        side_in(do_east, lv)
        unpack(lv, [PAD - HALO + 8 * r for r in wide])

        @pl.loop(1, STEPS + 1)
        def _(k):
            base = side_base(do_east, k)
            advance(k, lv, 0, base, 2, main)
            advance(k, lv, 0, PAD - HALO, len(wide), edge)
            keep(k, lv, 0, base, (2, 6), main)
            keep(k, lv, 0, PAD - HALO, [8 * r for r in wide], edge)

        finish(do_east, lv)
        for kind in (OLD, NEW):
            for tr in range(2):
                for r in range(row_tiles):
                    rows = slice(8 * r, 8 * r + 8)
                    end = state[STEPS, lv, kind, tr, tiles, PAD + 8 * r : PAD + 8 * r + 8, :]
                    for t in main:
                        here = state_v[kind, tr, lv, rows, t * LANES : (t + 1) * LANES]
                        if t == 0:
                            here = jnp.where(lane < HALO, roll(end, -HALO), here)
                        if t == tiles - 1:
                            here = jnp.where(lane >= LANES - HALO, roll(end, HALO), here)
                        outs[kind][tr, lv, rows, t * LANES : (t + 1) * LANES] = here

    for c in sum(eastward + westward, []):
        c.wait_send()
    up_main_copy.wait_send()

    @pl.when(not_self_east)
    def _():
        up_east_copy.wait_send()

    @pl.when(not_self_west)
    def _():
        up_west_copy.wait_send()

    @pl.when(not_bottom)
    def _():
        for c in down_copies:
            c.wait_send()


def solution(mesh):
    n_lon, n_lat = mesh.shape["lon"], mesh.shape["lat"]

    def shards(previous, current, east_speed, north_speed, east_mix, north_mix, sea_mask):
        columns, height = previous.shape[2:]
        tiles = height // LANES
        rows = columns + 2 * PAD
        field = jax.ShapeDtypeStruct(previous.shape, jnp.float32)
        f32 = jnp.float32
        done = pl.pallas_call(
            functools.partial(kernel, (n_lon, n_lat, columns, height)),
            out_shape=(pltpu.VMEM(previous.shape, f32), pltpu.VMEM(previous.shape, f32)),
            in_specs=[pl.BlockSpec(memory_space=pl.ANY)] * 7,
            out_specs=[pl.BlockSpec(memory_space=pltpu.VMEM)] * 2,
            scratch_shapes=[
                pltpu.VMEM(sea_mask.shape, sea_mask.dtype),
                pltpu.VMEM((2, *previous.shape), f32),
                pltpu.VMEM((4, *east_speed.shape), f32),
                pltpu.VMEM((STEPS + 1, 2, 2, 2, tiles + 1, rows, LANES), f32),
                pltpu.VMEM((2, 4, tiles + 1, rows, LANES), f32),
                pltpu.VMEM((2, 8, columns, LANES), f32),
                pltpu.VMEM((2, 2, tiles + 1, rows, LANES), f32),
                pltpu.VMEM((2, 2, 2, tiles + 1, rows, LANES), f32),
                pltpu.VMEM((2, 2, columns, LANES), f32),
                pltpu.VMEM((2, 2, rows, LANES), f32),
                pltpu.SemaphoreType.DMA((7,)),
                pltpu.SemaphoreType.DMA((2, 2, 7)),
                pltpu.SemaphoreType.DMA((2, 2, 7)),
                pltpu.SemaphoreType.DMA((2, 3)),
                pltpu.SemaphoreType.DMA((2, 3)),
                pltpu.SemaphoreType.DMA((2,)),
            ],
            compiler_params=pltpu.CompilerParams(
                collective_id=0, has_side_effects=True, vmem_limit_bytes=60 * 2**20
            ),
            cost_estimate=pl.CostEstimate(
                flops=30 * STEPS * previous.size, bytes_accessed=16 * previous.size, transcendentals=0
            ),
        )(previous, current, east_speed, north_speed, east_mix, north_mix, sea_mask)
        def hand_over(a, b, x, y, sems):
            copies = [
                pltpu.make_async_copy(src.at[tr], dst.at[tr], sems.at[i, tr])
                for i, (src, dst) in enumerate(((a, x), (b, y)))
                for tr in range(2)
            ]
            for c in copies:
                c.start()
            for c in copies:
                c.wait()

        return pl.pallas_call(
            hand_over,
            out_shape=(field, field),
            in_specs=[pl.BlockSpec(memory_space=pl.ANY)] * 2,
            out_specs=[pl.BlockSpec(memory_space=pl.ANY)] * 2,
            scratch_shapes=[pltpu.SemaphoreType.DMA((2, 2))],
            name="hand_over",
            compiler_params=pltpu.CompilerParams(vmem_limit_bytes=2**20),
        )(*done)


    return jax.shard_map(
        shards,
        mesh=mesh,
        in_specs=(
            P(None, None, "lon", "lat"),
            P(None, None, "lon", "lat"),
            P(None, "lon", "lat"),
            P(None, "lon", "lat"),
            P(None, "lon", "lat"),
            P(None, "lon", "lat"),
            P("lon", "lat"),
        ),
        out_specs=(P(None, None, "lon", "lat"), P(None, None, "lon", "lat")),
        check_vma=False,
    )
```

```python
import functools

import jax
import jax.numpy as jnp
from jax import lax
from jax.experimental import pallas as pl
from jax.experimental.pallas import tpu as pltpu
from jax.sharding import PartitionSpec as P

STEPS = 6
GAMMA = 0.1
MESH = pl.DeviceIdType.MESH

LANES = 128
PAD = 16
HALO = 2 * STEPS
SLOT = 16
UNIT = HALO
AHEAD = 5
OLD, NEW = 0, 1
ES, EM, NS, NM = range(4)
SCALES = (2.0 / 12.0, 2.0)


def kernel(sizes, *refs):
    n_lon, n_lat, columns, height = sizes
    (prev_h, cur_h, es_h, ns_h, em_h, nm_h, mask_h, lag_h, lat_h) = refs[:9]
    (mask_v, state_v, coef_v, state, coef, ends, div, held, pack, land) = refs[9:19]
    (in_sem, lon_send, lon_recv, lat_send, lat_recv, self_sem) = refs[19:]
    tiles = height // LANES
    ring = tiles + 1
    row_tiles = columns // 8
    own = pl.ds(PAD, columns)

    lon, lat = lax.axis_index("lon"), lax.axis_index("lat")
    east, west = lax.rem(lon + 1, n_lon), lax.rem(lon + n_lon - 1, n_lon)
    is_top, is_bottom = lat == n_lat - 1, lat == 0
    top = jnp.where(is_top, 1, 0)
    north, south = jnp.minimum(lat + 1, n_lat - 1), jnp.maximum(lat - 1, 0)
    up_main = jnp.where(is_top, n_lon - 1 - lon, lon)
    up_east = jnp.where(is_top, lax.rem(n_lon - lon, n_lon), east)
    up_west = jnp.where(is_top, lax.rem(2 * n_lon - 2 - lon, n_lon), west)
    self_east = jnp.logical_and(is_top, up_east == lon)
    self_west = jnp.logical_and(is_top, up_west == lon)
    not_self_east = jnp.logical_not(self_east)
    not_self_west = jnp.logical_not(self_west)
    not_bottom = jnp.logical_not(is_bottom)

    staged = [(mask_h, mask_v), (cur_h, state_v.at[NEW]), (prev_h, state_v.at[OLD])] + [
        (ref, coef_v.at[field]) for field, ref in enumerate((es_h, em_h, ns_h, nm_h))
    ]
    loads = [pltpu.make_async_copy(a, b, in_sem.at[i]) for i, (a, b) in enumerate(staged)]

    barrier = pltpu.get_barrier_semaphore()

    def greet(to_lon, to_lat):
        pl.semaphore_signal(
            barrier, inc=1, device_id={"lon": to_lon, "lat": to_lat}, device_id_type=MESH
        )

    greet(east, lat)
    greet(west, lat)
    greet(up_main, north)

    @pl.when(not_self_east)
    def _():
        greet(up_east, north)

    @pl.when(not_self_west)
    def _():
        greet(up_west, north)

    @pl.when(not_bottom)
    def _():
        greet(lon, south)
        greet(east, south)
        greet(west, south)

    for c in loads:
        c.start()

    lane = lax.broadcasted_iota(jnp.int32, (8, LANES), 1)
    sub = lax.broadcasted_iota(jnp.int32, (8, LANES), 0)

    def roll(x, shift):
        return pltpu.roll(x, shift % LANES, 1)

    def permute(x, source):
        return jnp.take_along_axis(x, source, axis=1)

    def exchange(tile):
        for bit in (1, 2, 4):
            keep = (lane & bit) == 0
            new = list(tile)
            for t in range(tiles):
                if not t & bit:
                    x, y = tile[t], tile[t + bit]
                    crossing = permute(jnp.where(keep, y, x), lane ^ bit)
                    new[t] = jnp.where(keep, x, crossing)
                    new[t + bit] = jnp.where(keep, crossing, y)
            tile = new
        return tile

    def lay_out(tile, target, end, r):
        rows = slice(PAD + 8 * r, PAD + 8 * r + 8)
        both = jnp.where(lane < LANES // 2, roll(tile[0], HALO), roll(tile[-1], -HALO))
        target[tiles, rows, :] = both
        end[8 * r : 8 * r + 8, :] = both
        for t, x in enumerate(exchange(tile)):
            target[t, rows, :] = x

    def block(r, t):
        return slice(8 * r, 8 * r + 8), slice(t * LANES, (t + 1) * LANES)

    def lay_state(lv):
        @pl.loop(0, 2)
        def _(kind):
            for r in range(row_tiles):
                wet = [mask_v[block(r, t)].astype(jnp.float32) for t in range(tiles)]
                for tr in range(2):
                    lay_out(
                        [state_v[kind, tr, lv, *block(r, t)] * wet[t] for t in range(tiles)],
                        state.at[0, lv, kind, tr],
                        ends.at[lv, 2 * kind + tr],
                        r,
                    )

    def lay_coef(lv):
        @pl.loop(0, 2)
        def _(pair):
            for j in range(2):
                for r in range(row_tiles):
                    lay_out(
                        [coef_v[2 * pair + j, lv, *block(r, t)] * SCALES[j] for t in range(tiles)],
                        coef.at[lv, 2 * pair + j],
                        ends.at[lv, 4 + 2 * pair + j],
                        r,
                    )

    slot_of_lane = lane // SLOT
    sign = jnp.where(is_top, -1.0, 1.0)

    def pack_ends(lv):
        for r in range(row_tiles):
            rows = slice(8 * r, 8 * r + 8)
            up = jnp.zeros((8, LANES), jnp.float32)
            down = jnp.zeros((8, LANES), jnp.float32)
            for s in range(8):
                here = slot_of_lane == s
                mine = ends[lv, s, rows, :]
                shift = (SLOT * s - (LANES - HALO - SLOT)) % LANES
                high = pltpu.roll(mine, shift + top, 1) if s in (4 + NS, 4 + NM) else roll(mine, shift)
                if s in (4 + ES, 4 + NS):
                    high = high * sign
                up = jnp.where(here, high, up)
                down = jnp.where(here, roll(mine, SLOT * s - HALO), down)
            pack[0, lv, rows, :] = up
            pack[1, lv, rows, :] = down

        @pl.when(is_top)
        def _():
            turned = []
            for r in range(row_tiles):
                x = permute(pack[0, lv, 8 * r : 8 * r + 8, :], lane ^ (SLOT - 1))
                for bit in (1, 2, 4):
                    x = jnp.where(
                        (sub & bit) == 0, pltpu.roll(x, 8 - bit, 0), pltpu.roll(x, bit, 0)
                    )
                turned.append(x)
            for r in range(row_tiles):
                pack[0, lv, 8 * r : 8 * r + 8, :] = turned[row_tiles - 1 - r]

    @pl.when(is_bottom)
    def _():
        land[0] = jnp.zeros(land.shape[1:], jnp.float32)

    def wait_peers():
        peers = 8 - jnp.where(is_bottom, 3, 0) - jnp.where(self_east, 1, 0) - jnp.where(self_west, 1, 0)
        pl.semaphore_wait(barrier, peers)

    own_rows = pl.ds(0, columns)
    last_rows, first_rows = pl.ds(columns - HALO, HALO), pl.ds(0, HALO)
    west_rows, east_rows = pl.ds(PAD - HALO, HALO), pl.ds(PAD + columns, HALO)

    def lat_copy(lv, out, src_rows, side, dst_rows, slot, to_lon, to_lat):
        return pltpu.make_async_remote_copy(
            src_ref=pack.at[out, lv, src_rows, :],
            dst_ref=land.at[side, lv, dst_rows, :],
            send_sem=lat_send.at[out, lv, slot],
            recv_sem=lat_recv.at[side, lv, slot],
            device_id={"lon": to_lon, "lat": to_lat},
            device_id_type=MESH,
        )

    def up_copies(lv):
        return [
            lat_copy(lv, 0, own_rows, top, own, 0, up_main, north),
            lat_copy(lv, 0, last_rows, top, west_rows, 1, up_east, north),
            lat_copy(lv, 0, first_rows, top, east_rows, 2, up_west, north),
        ]

    def down_copies(lv):
        return [
            lat_copy(lv, 1, own_rows, 1, own, 0, lon, south),
            lat_copy(lv, 1, last_rows, 1, west_rows, 1, east, south),
            lat_copy(lv, 1, first_rows, 1, east_rows, 2, west, south),
        ]

    def self_copies(lv):
        return [
            pltpu.make_async_copy(
                pack.at[0, lv, last_rows, :], land.at[1, lv, west_rows, :], self_sem.at[lv, 0]
            ),
            pltpu.make_async_copy(
                pack.at[0, lv, first_rows, :], land.at[1, lv, east_rows, :], self_sem.at[lv, 1]
            ),
        ]

    def each_way(to_main, to_east, to_west, own_east, own_west, to_south):
        to_main()
        pl.when(not_self_east)(to_east)
        pl.when(not_self_west)(to_west)
        pl.when(self_east)(own_east)
        pl.when(self_west)(own_west)
        pl.when(not_bottom)(to_south)

    def send_lat(lv):
        ups, downs, selves = up_copies(lv), down_copies(lv), self_copies(lv)

        def to_south():
            for c in downs:
                c.start()

        each_way(ups[0].start, ups[1].start, ups[2].start, selves[0].start, selves[1].start, to_south)

    def lat_in(lv):
        norths, selves = down_copies(lv), self_copies(lv)

        def from_south():
            for slot, (src, dst) in enumerate(
                ((own_rows, own), (last_rows, west_rows), (first_rows, east_rows))
            ):
                lat_copy(lv, 0, src, 0, dst, slot, lon, lat).wait_recv()

        each_way(
            norths[0].wait_recv, norths[1].wait_recv, norths[2].wait_recv,
            selves[0].wait, selves[1].wait, from_south,
        )

    def lat_sent(lv):
        ups, downs = up_copies(lv), down_copies(lv)

        def to_south():
            for c in downs:
                c.wait_send()

        def nothing():
            pass

        each_way(ups[0].wait_send, ups[1].wait_send, ups[2].wait_send, nothing, nothing, to_south)

    def lon_copies(way, lv, to_lon):
        def part(source, first, target, width):
            begin = first + (columns - width if way == 0 else 0)
            dst = PAD - width if way == 0 else PAD + columns
            return source.at[..., pl.ds(begin, width), :], target.at[..., pl.ds(dst, width), :]

        main_tiles = pl.ds(0, tiles)
        new, old = state.at[0, lv, NEW, :, main_tiles], state.at[0, lv, OLD, :, main_tiles]
        east_coef = coef.at[lv, pl.ds(ES, 2), main_tiles]
        north_coef = coef.at[lv, pl.ds(NS, 2), main_tiles]
        parts = [
            part(new, PAD, new, HALO),
            part(old, PAD, old, HALO - 1),
            part(east_coef, PAD, east_coef, HALO - 1 if way == 0 else HALO - 2),
            part(north_coef, PAD, north_coef, HALO - 2),
            part(ends.at[lv, pl.ds(0, 2)], 0, state.at[0, lv, OLD, :, tiles], HALO),
            part(ends.at[lv, pl.ds(2, 2)], 0, state.at[0, lv, NEW, :, tiles], HALO),
            part(ends.at[lv, pl.ds(4, 4)], 0, coef.at[lv, :, tiles], HALO),
        ]
        return [
            pltpu.make_async_remote_copy(
                src_ref=src,
                dst_ref=dst,
                send_sem=lon_send.at[way, lv, i],
                recv_sem=lon_recv.at[way, lv, i],
                device_id={"lon": to_lon, "lat": lat},
                device_id_type=MESH,
            )
            for i, (src, dst) in enumerate(parts)
        ]

    def send_lon(lv):
        for a, b in zip(lon_copies(0, lv, east), lon_copies(1, lv, west)):
            a.start()
            b.start()

    next_lane = jnp.where(lane >= LANES - 8, lane - (LANES - 9), lane + 8)
    last_lane = jnp.where(lane < 8, lane + (LANES - 9), lane - 8)

    def after(x):
        return [roll(x[0], -1)] if len(x) == 1 else x[1:] + [permute(x[0], next_lane)]

    def before(x):
        return [roll(x[0], 1)] if len(x) == 1 else [permute(x[-1], last_lane)] + x[:-1]

    def eastern(x):
        y = [pltpu.roll(a, 7, 0) for a in x]
        return [jnp.where(sub == 7, b, a) for a, b in zip(y, y[1:])] + y[-1:]

    def western(x):
        y = [pltpu.roll(a, 1, 0) for a in x]
        return y[:1] + [jnp.where(sub == 0, a, b) for a, b in zip(y, y[1:])]

    def advance(k, lv, slot, base, count, group):
        frames = [pl.ds(base + 8 * i, 8) for i in range(count)]
        old = state.at[k - 1, lv]
        for t in group:
            es = [coef[lv, ES, t, rows, :] for rows in frames]
            em = [coef[lv, EM, t, rows, :] for rows in frames]
            for tr in range(2):
                n = [old[NEW, tr, t, rows, :] for rows in frames]
                o = [old[OLD, tr, t, rows, :] for rows in frames]
                near = [a + b for a, b in zip(n, eastern(n))]
                flow = [
                    u * (8.0 * here - (a + b)) - v * (o1 - o0)
                    for u, v, here, a, b, o1, o0 in zip(
                        es, em, near, eastern(near), western(near), eastern(o), o
                    )
                ]
                for i, (a, b) in enumerate(zip(flow, western(flow))):
                    div[slot, tr, t, 8 * i : 8 * i + 8, :] = a - b
        for i, rows in enumerate(frames):
            mine = slice(8 * i, 8 * i + 8)
            for tr in range(2):
                n = [old[NEW, tr, t, rows, :] for t in group]
                o = [old[OLD, tr, t, rows, :] for t in group]
                near = [a + b for a, b in zip(n, after(n))]
                flow = [
                    coef[lv, NS, t, rows, :] * (8.0 * here - (a + b)) - coef[lv, NM, t, rows, :] * (o1 - o0)
                    for t, here, a, b, o1, o0 in zip(
                        group, near, after(near), before(near), after(o), o
                    )
                ]
                for j, (t, a, b) in enumerate(zip(group, flow, before(flow))):
                    fresh = o[j] - (div[slot, tr, t, mine, :] + (a - b))
                    held[slot, NEW, tr, t, mine, :] = fresh
                    held[slot, OLD, tr, t, mine, :] = (1.0 - 2.0 * GAMMA) * n[j] + GAMMA * (
                        o[j] + fresh
                    )

    def keep(k, lv, slot, base, windows, group):
        for kind in (NEW, OLD):
            for tr in range(2):
                for t in group:
                    for w in windows:
                        state[k, lv, kind, tr, t, pl.ds(base + w, 8), :] = held[
                            slot, kind, tr, t, w : w + 8, :
                        ]

    main, edge = list(range(tiles)), [tiles]

    def inner_place(u):
        k = jnp.where(u < 3, 1, jnp.where(u > 9, 6, (u - 3) // 2 + 2))
        j = jnp.where(u < 3, u, jnp.where(u < 9, lax.rem(u - 3, 2), 0))
        gap = jnp.where(u < 3, 8, 20 - 4 * k)
        return k, PAD + jnp.minimum(2 * k, 10) + j * gap

    def inner_unit(u):
        k, r0 = inner_place(u)
        for lv in range(2):
            advance(k, lv, lv, r0 - 2, 2, main)
        for lv in range(2):
            keep(k, lv, lv, r0 - 2, (2, 6), main)

    place = lax.rem(lon, n_lon // 2)
    patient = jnp.logical_or(place == 0, jnp.logical_and(is_top, place < n_lon // 4))
    ahead = jnp.where(patient, AHEAD, 0)
    for c in loads:
        c.wait()

    @pl.loop(0, 2)
    def _(lv):
        lay_state(lv)
        lay_coef(lv)
        pack_ends(lv)

        @pl.when(jnp.logical_not(patient))
        def _():
            @pl.when(lv == 0)
            def _():
                wait_peers()

            send_lat(lv)
            send_lon(lv)

    @pl.when(patient)
    def _():
        @pl.loop(0, AHEAD)
        def _(u):
            inner_unit(u)

        wait_peers()

        @pl.loop(0, 2)
        def _(lv):
            send_lat(lv)
            send_lon(lv)

    @pl.loop(ahead, 11)
    def _(u):
        inner_unit(u)

    even = lax.rem(lon, 2) == 0
    outs = (lag_h, lat_h)
    wide = range((columns + 2 * HALO) // 8)

    def side_in(do_east, lv):
        @pl.when(do_east)
        def _():
            for c in lon_copies(1, lv, west):
                c.wait_recv()

        @pl.when(jnp.logical_not(do_east))
        def _():
            for c in lon_copies(0, lv, east):
                c.wait_recv()

    def side_base(do_east, k):
        return jnp.where(do_east, PAD + columns - 2 * k, PAD + 2 * k - UNIT) - 2

    def finish(do_east, lv):
        first = pl.multiple_of(jnp.where(do_east, columns // 2, 0), 16)

        @pl.loop(0, 2)
        def _(kind_no):
            for r in range(2):
                rows = pl.ds(pl.multiple_of(first + 8 * r, 8), 8)
                source = pl.ds(pl.multiple_of(PAD + first + 8 * r, 8), 8)
                for tr in range(2):
                    tile = exchange([state[STEPS, lv, kind_no, tr, t, source, :] for t in main])
                    for t in main:
                        state_v[kind_no, tr, lv, rows, t * LANES : (t + 1) * LANES] = tile[t]

    @pl.loop(0, 2)
    def _(lv):
        side_in(even, lv)

        @pl.loop(1, STEPS + 1)
        def _(k):
            base = side_base(even, k)
            advance(k, lv, 0, base, 2, main)
            keep(k, lv, 0, base, (2, 6), main)

        finish(even, lv)

    def unpack(lv, begins):
        done = []
        for begin in begins:
            rows = pl.ds(begin, 8)
            for f in range(8):
                source = pl.ds(begin + top, 8) if f in (4 + ES, 4 + EM) else rows
                north_part = roll(land[1, lv, source, :], LANES - HALO - SLOT * f)
                south_part = roll(land[0, lv, rows, :], HALO - SLOT - SLOT * f)
                if f < 4:
                    target = state.at[0, lv, f // 2, f % 2, tiles]
                else:
                    target = coef.at[lv, f - 4, tiles]
                inside = jnp.where(lane < HALO, south_part, target[rows, :])
                done.append((target, rows, jnp.where(lane >= LANES - HALO, north_part, inside)))
        for target, rows, value in done:
            target[rows, :] = value

    @pl.loop(0, 2)
    def _(lv):
        do_east = jnp.logical_not(even)
        lat_in(lv)
        side_in(do_east, lv)
        unpack(lv, [PAD - HALO + 8 * r for r in wide])

        @pl.loop(1, STEPS + 1)
        def _(k):
            base = side_base(do_east, k)
            advance(k, lv, 0, base, 2, main)
            advance(k, lv, 0, PAD - HALO, len(wide), edge)
            keep(k, lv, 0, base, (2, 6), main)
            keep(k, lv, 0, PAD - HALO, [8 * r for r in wide], edge)

        finish(do_east, lv)
        for kind in (OLD, NEW):
            for tr in range(2):
                for r in range(row_tiles):
                    rows = slice(8 * r, 8 * r + 8)
                    end = state[STEPS, lv, kind, tr, tiles, PAD + 8 * r : PAD + 8 * r + 8, :]
                    for t in main:
                        here = state_v[kind, tr, lv, rows, t * LANES : (t + 1) * LANES]
                        if t == 0:
                            here = jnp.where(lane < HALO, roll(end, -HALO), here)
                        if t == tiles - 1:
                            here = jnp.where(lane >= LANES - HALO, roll(end, HALO), here)
                        outs[kind][tr, lv, rows, t * LANES : (t + 1) * LANES] = here

    @pl.loop(0, 2)
    def _(lv):
        for c in lon_copies(0, lv, east) + lon_copies(1, lv, west):
            c.wait_send()
        lat_sent(lv)


def solution(mesh):
    n_lon, n_lat = mesh.shape["lon"], mesh.shape["lat"]

    def shards(previous, current, east_speed, north_speed, east_mix, north_mix, sea_mask):
        columns, height = previous.shape[2:]
        tiles = height // LANES
        rows = columns + 2 * PAD
        field = jax.ShapeDtypeStruct(previous.shape, jnp.float32)
        f32 = jnp.float32
        done = pl.pallas_call(
            functools.partial(kernel, (n_lon, n_lat, columns, height)),
            out_shape=(pltpu.VMEM(previous.shape, f32), pltpu.VMEM(previous.shape, f32)),
            in_specs=[pl.BlockSpec(memory_space=pl.ANY)] * 7,
            out_specs=[pl.BlockSpec(memory_space=pltpu.VMEM)] * 2,
            scratch_shapes=[
                pltpu.VMEM(sea_mask.shape, sea_mask.dtype),
                pltpu.VMEM((2, *previous.shape), f32),
                pltpu.VMEM((4, *east_speed.shape), f32),
                pltpu.VMEM((STEPS + 1, 2, 2, 2, tiles + 1, rows, LANES), f32),
                pltpu.VMEM((2, 4, tiles + 1, rows, LANES), f32),
                pltpu.VMEM((2, 8, columns, LANES), f32),
                pltpu.VMEM((2, 2, tiles + 1, rows, LANES), f32),
                pltpu.VMEM((2, 2, 2, tiles + 1, rows, LANES), f32),
                pltpu.VMEM((2, 2, columns, LANES), f32),
                pltpu.VMEM((2, 2, rows, LANES), f32),
                pltpu.SemaphoreType.DMA((7,)),
                pltpu.SemaphoreType.DMA((2, 2, 7)),
                pltpu.SemaphoreType.DMA((2, 2, 7)),
                pltpu.SemaphoreType.DMA((2, 2, 3)),
                pltpu.SemaphoreType.DMA((2, 2, 3)),
                pltpu.SemaphoreType.DMA((2, 2)),
            ],
            compiler_params=pltpu.CompilerParams(
                collective_id=0, has_side_effects=True, vmem_limit_bytes=60 * 2**20
            ),
            cost_estimate=pl.CostEstimate(
                flops=30 * STEPS * previous.size, bytes_accessed=16 * previous.size, transcendentals=0
            ),
        )(previous, current, east_speed, north_speed, east_mix, north_mix, sea_mask)
        def hand_over(a, b, x, y, sems):
            copies = [
                pltpu.make_async_copy(src.at[tr], dst.at[tr], sems.at[i, tr])
                for i, (src, dst) in enumerate(((a, x), (b, y)))
                for tr in range(2)
            ]
            for c in copies:
                c.start()
            for c in copies:
                c.wait()

        return pl.pallas_call(
            hand_over,
            out_shape=(field, field),
            in_specs=[pl.BlockSpec(memory_space=pl.ANY)] * 2,
            out_specs=[pl.BlockSpec(memory_space=pl.ANY)] * 2,
            scratch_shapes=[pltpu.SemaphoreType.DMA((2, 2))],
            name="hand_over",
            compiler_params=pltpu.CompilerParams(vmem_limit_bytes=2**20),
        )(*done)


    return jax.shard_map(
        shards,
        mesh=mesh,
        in_specs=(
            P(None, None, "lon", "lat"),
            P(None, None, "lon", "lat"),
            P(None, "lon", "lat"),
            P(None, "lon", "lat"),
            P(None, "lon", "lat"),
            P(None, "lon", "lat"),
            P("lon", "lat"),
        ),
        out_specs=(P(None, None, "lon", "lat"), P(None, None, "lon", "lat")),
        check_vma=False,
    )
```

```python
import functools

import jax
import jax.numpy as jnp
from jax import lax
from jax.experimental import pallas as pl
from jax.experimental.pallas import tpu as pltpu
from jax.sharding import PartitionSpec as P

STEPS = 6
GAMMA = 0.1
MESH = pl.DeviceIdType.MESH

LANES = 128
PAD = 16
HALO = 2 * STEPS
SLOT = 16
UNIT = HALO
FIRST = 5
OLD, NEW = 0, 1
ES, EM, NS, NM = range(4)
SCALES = (2.0 / 12.0, 2.0)


def kernel(sizes, *refs):
    n_lon, n_lat, columns, height = sizes
    (prev_h, cur_h, es_h, ns_h, em_h, nm_h, mask_h, lag_h, lat_h) = refs[:9]
    (mask_v, state_v, coef_v, state, coef, ends, div, held, pack, land) = refs[9:19]
    (in_sem, lon_send, lon_recv, lat_send, lat_recv, self_sem) = refs[19:]
    tiles = height // LANES
    ring = tiles + 1
    row_tiles = columns // 8
    own = pl.ds(PAD, columns)

    lon, lat = lax.axis_index("lon"), lax.axis_index("lat")
    east, west = lax.rem(lon + 1, n_lon), lax.rem(lon + n_lon - 1, n_lon)
    is_top, is_bottom = lat == n_lat - 1, lat == 0
    top = jnp.where(is_top, 1, 0)
    north, south = jnp.minimum(lat + 1, n_lat - 1), jnp.maximum(lat - 1, 0)
    up_main = jnp.where(is_top, n_lon - 1 - lon, lon)
    up_east = jnp.where(is_top, lax.rem(n_lon - lon, n_lon), east)
    up_west = jnp.where(is_top, lax.rem(2 * n_lon - 2 - lon, n_lon), west)
    self_east = jnp.logical_and(is_top, up_east == lon)
    self_west = jnp.logical_and(is_top, up_west == lon)
    not_self_east = jnp.logical_not(self_east)
    not_self_west = jnp.logical_not(self_west)
    not_bottom = jnp.logical_not(is_bottom)

    staged = [(mask_h, mask_v), (cur_h, state_v.at[NEW]), (prev_h, state_v.at[OLD])] + [
        (ref, coef_v.at[field]) for field, ref in enumerate((es_h, em_h, ns_h, nm_h))
    ]
    loads = [pltpu.make_async_copy(a, b, in_sem.at[i]) for i, (a, b) in enumerate(staged)]

    barrier = pltpu.get_barrier_semaphore()

    def greet(to_lon, to_lat):
        pl.semaphore_signal(
            barrier, inc=1, device_id={"lon": to_lon, "lat": to_lat}, device_id_type=MESH
        )

    greet(east, lat)
    greet(west, lat)
    greet(up_main, north)

    @pl.when(not_self_east)
    def _():
        greet(up_east, north)

    @pl.when(not_self_west)
    def _():
        greet(up_west, north)

    @pl.when(not_bottom)
    def _():
        greet(lon, south)
        greet(east, south)
        greet(west, south)

    for c in loads:
        c.start()

    lane = lax.broadcasted_iota(jnp.int32, (8, LANES), 1)
    sub = lax.broadcasted_iota(jnp.int32, (8, LANES), 0)

    def roll(x, shift):
        return pltpu.roll(x, shift % LANES, 1)

    def permute(x, source):
        return jnp.take_along_axis(x, source, axis=1)

    def exchange(tile):
        for bit in (1, 2, 4):
            keep = (lane & bit) == 0
            new = list(tile)
            for t in range(tiles):
                if not t & bit:
                    x, y = tile[t], tile[t + bit]
                    crossing = permute(jnp.where(keep, y, x), lane ^ bit)
                    new[t] = jnp.where(keep, x, crossing)
                    new[t + bit] = jnp.where(keep, crossing, y)
            tile = new
        return tile

    def lay_out(tile, target, end, r):
        rows = slice(PAD + 8 * r, PAD + 8 * r + 8)
        both = jnp.where(lane < LANES // 2, roll(tile[0], HALO), roll(tile[-1], -HALO))
        target[tiles, rows, :] = both
        end[8 * r : 8 * r + 8, :] = both
        for t, x in enumerate(exchange(tile)):
            target[t, rows, :] = x

    def block(r, t):
        return slice(8 * r, 8 * r + 8), slice(t * LANES, (t + 1) * LANES)

    def lay_state(lv):
        @pl.loop(0, 2)
        def _(kind):
            for r in range(row_tiles):
                wet = [mask_v[block(r, t)].astype(jnp.float32) for t in range(tiles)]
                for tr in range(2):
                    lay_out(
                        [state_v[kind, tr, lv, *block(r, t)] * wet[t] for t in range(tiles)],
                        state.at[0, lv, kind, tr],
                        ends.at[lv, 2 * kind + tr],
                        r,
                    )

    def lay_coef(lv):
        @pl.loop(0, 2)
        def _(pair):
            for j in range(2):
                for r in range(row_tiles):
                    lay_out(
                        [coef_v[2 * pair + j, lv, *block(r, t)] * SCALES[j] for t in range(tiles)],
                        coef.at[lv, 2 * pair + j],
                        ends.at[lv, 4 + 2 * pair + j],
                        r,
                    )

    slot_of_lane = lane // SLOT
    sign = jnp.where(is_top, -1.0, 1.0)

    def pack_ends(lv):
        for r in range(row_tiles):
            rows = slice(8 * r, 8 * r + 8)
            up = jnp.zeros((8, LANES), jnp.float32)
            down = jnp.zeros((8, LANES), jnp.float32)
            for s in range(8):
                here = slot_of_lane == s
                mine = ends[lv, s, rows, :]
                shift = (SLOT * s - (LANES - HALO - SLOT)) % LANES
                high = pltpu.roll(mine, shift + top, 1) if s in (4 + NS, 4 + NM) else roll(mine, shift)
                if s in (4 + ES, 4 + NS):
                    high = high * sign
                up = jnp.where(here, high, up)
                down = jnp.where(here, roll(mine, SLOT * s - HALO), down)
            pack[0, lv, rows, :] = up
            pack[1, lv, rows, :] = down

        @pl.when(is_top)
        def _():
            turned = []
            for r in range(row_tiles):
                x = permute(pack[0, lv, 8 * r : 8 * r + 8, :], lane ^ (SLOT - 1))
                for bit in (1, 2, 4):
                    x = jnp.where(
                        (sub & bit) == 0, pltpu.roll(x, 8 - bit, 0), pltpu.roll(x, bit, 0)
                    )
                turned.append(x)
            for r in range(row_tiles):
                pack[0, lv, 8 * r : 8 * r + 8, :] = turned[row_tiles - 1 - r]

    @pl.when(is_bottom)
    def _():
        land[0] = jnp.zeros(land.shape[1:], jnp.float32)

    def wait_peers():
        peers = 8 - jnp.where(is_bottom, 3, 0) - jnp.where(self_east, 1, 0) - jnp.where(self_west, 1, 0)
        pl.semaphore_wait(barrier, peers)

    own_rows = pl.ds(0, columns)
    last_rows, first_rows = pl.ds(columns - HALO, HALO), pl.ds(0, HALO)
    west_rows, east_rows = pl.ds(PAD - HALO, HALO), pl.ds(PAD + columns, HALO)

    def lat_copy(lv, out, src_rows, side, dst_rows, slot, to_lon, to_lat):
        return pltpu.make_async_remote_copy(
            src_ref=pack.at[out, lv, src_rows, :],
            dst_ref=land.at[side, lv, dst_rows, :],
            send_sem=lat_send.at[out, lv, slot],
            recv_sem=lat_recv.at[side, lv, slot],
            device_id={"lon": to_lon, "lat": to_lat},
            device_id_type=MESH,
        )

    def up_copies(lv):
        return [
            lat_copy(lv, 0, own_rows, top, own, 0, up_main, north),
            lat_copy(lv, 0, last_rows, top, west_rows, 1, up_east, north),
            lat_copy(lv, 0, first_rows, top, east_rows, 2, up_west, north),
        ]

    def down_copies(lv):
        return [
            lat_copy(lv, 1, own_rows, 1, own, 0, lon, south),
            lat_copy(lv, 1, last_rows, 1, west_rows, 1, east, south),
            lat_copy(lv, 1, first_rows, 1, east_rows, 2, west, south),
        ]

    def self_copies(lv):
        return [
            pltpu.make_async_copy(
                pack.at[0, lv, last_rows, :], land.at[1, lv, west_rows, :], self_sem.at[lv, 0]
            ),
            pltpu.make_async_copy(
                pack.at[0, lv, first_rows, :], land.at[1, lv, east_rows, :], self_sem.at[lv, 1]
            ),
        ]

    def each_way(to_main, to_east, to_west, own_east, own_west, to_south):
        to_main()
        pl.when(not_self_east)(to_east)
        pl.when(not_self_west)(to_west)
        pl.when(self_east)(own_east)
        pl.when(self_west)(own_west)
        pl.when(not_bottom)(to_south)

    def send_lat(lv):
        ups, downs, selves = up_copies(lv), down_copies(lv), self_copies(lv)

        def to_south():
            for c in downs:
                c.start()

        each_way(ups[0].start, ups[1].start, ups[2].start, selves[0].start, selves[1].start, to_south)

    def lat_in(lv):
        norths, selves = down_copies(lv), self_copies(lv)

        def from_south():
            for slot, (src, dst) in enumerate(
                ((own_rows, own), (last_rows, west_rows), (first_rows, east_rows))
            ):
                lat_copy(lv, 0, src, 0, dst, slot, lon, lat).wait_recv()

        each_way(
            norths[0].wait_recv, norths[1].wait_recv, norths[2].wait_recv,
            selves[0].wait, selves[1].wait, from_south,
        )

    def lat_sent(lv):
        ups, downs = up_copies(lv), down_copies(lv)

        def to_south():
            for c in downs:
                c.wait_send()

        def nothing():
            pass

        each_way(ups[0].wait_send, ups[1].wait_send, ups[2].wait_send, nothing, nothing, to_south)

    def lon_copies(way, lv, to_lon):
        main_tiles = pl.ds(0, tiles)

        def part(source, first, target, width, skip=0):
            begin = first + (columns - skip - width if way == 0 else skip)
            dst = PAD - skip - width if way == 0 else PAD + columns + skip
            return source.at[..., pl.ds(begin, width), :], target.at[..., pl.ds(dst, width), :]

        def main_part(ref, width, skip=0):
            return part(ref, PAD, ref, width, skip)

        parts = [
            main_part(state.at[k, lv, kind, :, main_tiles], width, 2 * k)
            for k in range(3)
            for kind, width in ((NEW, 4), (OLD, 3))
        ] + [
            main_part(coef.at[lv, pl.ds(ES, 2), main_tiles], 7 if way == 0 else 6),
            main_part(coef.at[lv, pl.ds(NS, 2), main_tiles], 6),
            part(ends.at[lv, pl.ds(0, 2)], 0, state.at[0, lv, OLD, :, tiles], HALO),
            part(ends.at[lv, pl.ds(2, 2)], 0, state.at[0, lv, NEW, :, tiles], HALO),
            part(ends.at[lv, pl.ds(4, 4)], 0, coef.at[lv, :, tiles], HALO),
        ]
        return [
            pltpu.make_async_remote_copy(
                src_ref=src,
                dst_ref=dst,
                send_sem=lon_send.at[way, lv, i],
                recv_sem=lon_recv.at[way, lv, i],
                device_id={"lon": to_lon, "lat": lat},
                device_id_type=MESH,
            )
            for i, (src, dst) in enumerate(parts)
        ]

    def send_lon(lv, parts):
        a, b = lon_copies(0, lv, east), lon_copies(1, lv, west)
        for i in parts:
            a[i].start()
            b[i].start()

    AT_ONCE, STEPPED = (0, 1, 6, 7, 8, 9, 10), (2, 3, 4, 5)

    next_lane = jnp.where(lane >= LANES - 8, lane - (LANES - 9), lane + 8)
    last_lane = jnp.where(lane < 8, lane + (LANES - 9), lane - 8)

    def after(x):
        return [roll(x[0], -1)] if len(x) == 1 else x[1:] + [permute(x[0], next_lane)]

    def before(x):
        return [roll(x[0], 1)] if len(x) == 1 else [permute(x[-1], last_lane)] + x[:-1]

    def eastern(x):
        y = [pltpu.roll(a, 7, 0) for a in x]
        return [jnp.where(sub == 7, b, a) for a, b in zip(y, y[1:])] + y[-1:]

    def western(x):
        y = [pltpu.roll(a, 1, 0) for a in x]
        return y[:1] + [jnp.where(sub == 0, a, b) for a, b in zip(y, y[1:])]

    def advance(k, lv, slot, base, count, group):
        frames = [pl.ds(base + 8 * i, 8) for i in range(count)]
        old = state.at[k - 1, lv]
        for t in group:
            es = [coef[lv, ES, t, rows, :] for rows in frames]
            em = [coef[lv, EM, t, rows, :] for rows in frames]
            for tr in range(2):
                n = [old[NEW, tr, t, rows, :] for rows in frames]
                o = [old[OLD, tr, t, rows, :] for rows in frames]
                near = [a + b for a, b in zip(n, eastern(n))]
                flow = [
                    u * (8.0 * here - (a + b)) - v * (o1 - o0)
                    for u, v, here, a, b, o1, o0 in zip(
                        es, em, near, eastern(near), western(near), eastern(o), o
                    )
                ]
                for i, (a, b) in enumerate(zip(flow, western(flow))):
                    div[slot, tr, t, 8 * i : 8 * i + 8, :] = a - b
        for i, rows in enumerate(frames):
            mine = slice(8 * i, 8 * i + 8)
            for tr in range(2):
                n = [old[NEW, tr, t, rows, :] for t in group]
                o = [old[OLD, tr, t, rows, :] for t in group]
                near = [a + b for a, b in zip(n, after(n))]
                flow = [
                    coef[lv, NS, t, rows, :] * (8.0 * here - (a + b)) - coef[lv, NM, t, rows, :] * (o1 - o0)
                    for t, here, a, b, o1, o0 in zip(
                        group, near, after(near), before(near), after(o), o
                    )
                ]
                for j, (t, a, b) in enumerate(zip(group, flow, before(flow))):
                    fresh = o[j] - (div[slot, tr, t, mine, :] + (a - b))
                    held[slot, NEW, tr, t, mine, :] = fresh
                    held[slot, OLD, tr, t, mine, :] = (1.0 - 2.0 * GAMMA) * n[j] + GAMMA * (
                        o[j] + fresh
                    )

    def keep(k, lv, slot, base, windows, group):
        for kind in (NEW, OLD):
            for tr in range(2):
                for t in group:
                    for w in windows:
                        state[k, lv, kind, tr, t, pl.ds(base + w, 8), :] = held[
                            slot, kind, tr, t, w : w + 8, :
                        ]

    main, edge = list(range(tiles)), [tiles]

    def inner_place(u):
        k = jnp.where(u < 3, 1, jnp.where(u > 9, 6, (u - 3) // 2 + 2))
        j = jnp.where(u < 3, u, jnp.where(u < 9, lax.rem(u - 3, 2), 0))
        gap = jnp.where(u < 3, 8, 20 - 4 * k)
        return k, PAD + jnp.minimum(2 * k, 10) + j * gap

    def inner_unit(u, levels):
        k, r0 = inner_place(u)
        for slot, lv in enumerate(levels):
            advance(k, lv, slot, r0 - 2, 2, main)
        for slot, lv in enumerate(levels):
            keep(k, lv, slot, r0 - 2, (2, 6), main)

    place = lax.rem(lon, n_lon // 2)
    patient = jnp.logical_or(place == 0, jnp.logical_and(is_top, place < n_lon // 4))
    for c in loads:
        c.wait()

    @pl.loop(0, 2)
    def _(lv):
        lay_state(lv)
        lay_coef(lv)
        pack_ends(lv)

        @pl.when(jnp.logical_not(patient))
        def _():
            @pl.when(lv == 0)
            def _():
                wait_peers()

            send_lat(lv)
            send_lon(lv, AT_ONCE)

        @pl.loop(0, FIRST)
        def _(u):
            inner_unit(u, [lv])

        @pl.when(jnp.logical_not(patient))
        def _():
            send_lon(lv, STEPPED)

    @pl.when(patient)
    def _():
        wait_peers()

        @pl.loop(0, 2)
        def _(lv):
            send_lat(lv)
            send_lon(lv, AT_ONCE + STEPPED)

    @pl.loop(FIRST, 11)
    def _(u):
        inner_unit(u, range(2))

    even = lax.rem(lon, 2) == 0
    outs = (lag_h, lat_h)
    wide = range((columns + 2 * HALO) // 8)

    def side_in(do_east, lv):
        @pl.when(do_east)
        def _():
            for c in lon_copies(1, lv, west):
                c.wait_recv()
            for c in lon_copies(0, lv, east):
                c.wait_send()

        @pl.when(jnp.logical_not(do_east))
        def _():
            for c in lon_copies(0, lv, east):
                c.wait_recv()
            for c in lon_copies(1, lv, west):
                c.wait_send()

    def side_base(do_east, k):
        west_base = jnp.maximum(2 * k - UNIT, -2 * k)
        return jnp.where(do_east, PAD + columns - UNIT - west_base, PAD + west_base) - 2

    def finish(do_east, lv):
        first = pl.multiple_of(jnp.where(do_east, columns // 2, 0), 16)

        @pl.loop(0, 2)
        def _(kind_no):
            for r in range(2):
                rows = pl.ds(pl.multiple_of(first + 8 * r, 8), 8)
                source = pl.ds(pl.multiple_of(PAD + first + 8 * r, 8), 8)
                for tr in range(2):
                    tile = exchange([state[STEPS, lv, kind_no, tr, t, source, :] for t in main])
                    for t in main:
                        state_v[kind_no, tr, lv, rows, t * LANES : (t + 1) * LANES] = tile[t]

    @pl.loop(0, 2)
    def _(lv):
        side_in(even, lv)

        @pl.loop(1, STEPS + 1)
        def _(k):
            base = side_base(even, k)
            advance(k, lv, 0, base, 2, main)
            keep(k, lv, 0, base, (2, 6), main)

        finish(even, lv)

    def unpack(lv, begins):
        done = []
        for begin in begins:
            rows = pl.ds(begin, 8)
            for f in range(8):
                source = pl.ds(begin + top, 8) if f in (4 + ES, 4 + EM) else rows
                north_part = roll(land[1, lv, source, :], LANES - HALO - SLOT * f)
                south_part = roll(land[0, lv, rows, :], HALO - SLOT - SLOT * f)
                if f < 4:
                    target = state.at[0, lv, f // 2, f % 2, tiles]
                else:
                    target = coef.at[lv, f - 4, tiles]
                inside = jnp.where(lane < HALO, south_part, target[rows, :])
                done.append((target, rows, jnp.where(lane >= LANES - HALO, north_part, inside)))
        for target, rows, value in done:
            target[rows, :] = value

    @pl.loop(0, 2)
    def _(lv):
        do_east = jnp.logical_not(even)
        lat_in(lv)
        side_in(do_east, lv)
        unpack(lv, [PAD - HALO + 8 * r for r in wide])

        @pl.loop(1, STEPS + 1)
        def _(k):
            base = side_base(do_east, k)
            advance(k, lv, 0, base, 2, main)
            advance(k, lv, 0, PAD - HALO, len(wide), edge)
            keep(k, lv, 0, base, (2, 6), main)
            keep(k, lv, 0, PAD - HALO, [8 * r for r in wide], edge)

        finish(do_east, lv)
        for kind in (OLD, NEW):
            for tr in range(2):
                for r in range(row_tiles):
                    rows = slice(8 * r, 8 * r + 8)
                    end = state[STEPS, lv, kind, tr, tiles, PAD + 8 * r : PAD + 8 * r + 8, :]
                    for t in main:
                        here = state_v[kind, tr, lv, rows, t * LANES : (t + 1) * LANES]
                        if t == 0:
                            here = jnp.where(lane < HALO, roll(end, -HALO), here)
                        if t == tiles - 1:
                            here = jnp.where(lane >= LANES - HALO, roll(end, HALO), here)
                        outs[kind][tr, lv, rows, t * LANES : (t + 1) * LANES] = here

    @pl.loop(0, 2)
    def _(lv):
        lat_sent(lv)


def solution(mesh):
    n_lon, n_lat = mesh.shape["lon"], mesh.shape["lat"]

    def shards(previous, current, east_speed, north_speed, east_mix, north_mix, sea_mask):
        columns, height = previous.shape[2:]
        tiles = height // LANES
        rows = columns + 2 * PAD
        field = jax.ShapeDtypeStruct(previous.shape, jnp.float32)
        f32 = jnp.float32
        done = pl.pallas_call(
            functools.partial(kernel, (n_lon, n_lat, columns, height)),
            out_shape=(pltpu.VMEM(previous.shape, f32), pltpu.VMEM(previous.shape, f32)),
            in_specs=[pl.BlockSpec(memory_space=pl.ANY)] * 7,
            out_specs=[pl.BlockSpec(memory_space=pltpu.VMEM)] * 2,
            scratch_shapes=[
                pltpu.VMEM(sea_mask.shape, sea_mask.dtype),
                pltpu.VMEM((2, *previous.shape), f32),
                pltpu.VMEM((4, *east_speed.shape), f32),
                pltpu.VMEM((STEPS + 1, 2, 2, 2, tiles + 1, rows, LANES), f32),
                pltpu.VMEM((2, 4, tiles + 1, rows, LANES), f32),
                pltpu.VMEM((2, 8, columns, LANES), f32),
                pltpu.VMEM((2, 2, tiles + 1, rows, LANES), f32),
                pltpu.VMEM((2, 2, 2, tiles + 1, rows, LANES), f32),
                pltpu.VMEM((2, 2, columns, LANES), f32),
                pltpu.VMEM((2, 2, rows, LANES), f32),
                pltpu.SemaphoreType.DMA((7,)),
                pltpu.SemaphoreType.DMA((2, 2, 11)),
                pltpu.SemaphoreType.DMA((2, 2, 11)),
                pltpu.SemaphoreType.DMA((2, 2, 3)),
                pltpu.SemaphoreType.DMA((2, 2, 3)),
                pltpu.SemaphoreType.DMA((2, 2)),
            ],
            compiler_params=pltpu.CompilerParams(
                collective_id=0, has_side_effects=True, vmem_limit_bytes=60 * 2**20
            ),
            cost_estimate=pl.CostEstimate(
                flops=30 * STEPS * previous.size, bytes_accessed=16 * previous.size, transcendentals=0
            ),
        )(previous, current, east_speed, north_speed, east_mix, north_mix, sea_mask)
        def hand_over(a, b, x, y, sems):
            copies = [
                pltpu.make_async_copy(src.at[tr], dst.at[tr], sems.at[i, tr])
                for i, (src, dst) in enumerate(((a, x), (b, y)))
                for tr in range(2)
            ]
            for c in copies:
                c.start()
            for c in copies:
                c.wait()

        return pl.pallas_call(
            hand_over,
            out_shape=(field, field),
            in_specs=[pl.BlockSpec(memory_space=pl.ANY)] * 2,
            out_specs=[pl.BlockSpec(memory_space=pl.ANY)] * 2,
            scratch_shapes=[pltpu.SemaphoreType.DMA((2, 2))],
            name="hand_over",
            compiler_params=pltpu.CompilerParams(vmem_limit_bytes=2**20),
        )(*done)


    return jax.shard_map(
        shards,
        mesh=mesh,
        in_specs=(
            P(None, None, "lon", "lat"),
            P(None, None, "lon", "lat"),
            P(None, "lon", "lat"),
            P(None, "lon", "lat"),
            P(None, "lon", "lat"),
            P(None, "lon", "lat"),
            P("lon", "lat"),
        ),
        out_specs=(P(None, None, "lon", "lat"), P(None, None, "lon", "lat")),
        check_vma=False,
    )
```

```python
import functools

import jax
import jax.numpy as jnp
from jax import lax
from jax.experimental import pallas as pl
from jax.experimental.pallas import tpu as pltpu
from jax.sharding import PartitionSpec as P

STEPS = 6
GAMMA = 0.1
MESH = pl.DeviceIdType.MESH

LANES = 128
PAD = 16
HALO = 2 * STEPS
SLOT = 16
UNIT = HALO
FIRST = 5
OLD, NEW = 0, 1
ES, EM, NS, NM = range(4)
SCALES = (2.0 / 12.0, 2.0)


def kernel(sizes, *refs):
    n_lon, n_lat, columns, height = sizes
    (prev_h, cur_h, es_h, ns_h, em_h, nm_h, mask_h, lag_h, lat_h) = refs[:9]
    (mask_v, state_v, coef_v, state, coef, ends, div, held, pack, land) = refs[9:19]
    (in_sem, lon_send, lon_recv, lat_send, lat_recv, self_sem) = refs[19:]
    tiles = height // LANES
    ring = tiles + 1
    row_tiles = columns // 8
    own = pl.ds(PAD, columns)

    lon, lat = lax.axis_index("lon"), lax.axis_index("lat")
    east, west = lax.rem(lon + 1, n_lon), lax.rem(lon + n_lon - 1, n_lon)
    is_top, is_bottom = lat == n_lat - 1, lat == 0
    top = jnp.where(is_top, 1, 0)
    north, south = jnp.minimum(lat + 1, n_lat - 1), jnp.maximum(lat - 1, 0)
    up_main = jnp.where(is_top, n_lon - 1 - lon, lon)
    up_east = jnp.where(is_top, lax.rem(n_lon - lon, n_lon), east)
    up_west = jnp.where(is_top, lax.rem(2 * n_lon - 2 - lon, n_lon), west)
    self_east = jnp.logical_and(is_top, up_east == lon)
    self_west = jnp.logical_and(is_top, up_west == lon)
    not_self_east = jnp.logical_not(self_east)
    not_self_west = jnp.logical_not(self_west)
    not_bottom = jnp.logical_not(is_bottom)

    staged = [(mask_h, mask_v), (cur_h, state_v.at[NEW]), (prev_h, state_v.at[OLD])] + [
        (ref, coef_v.at[field]) for field, ref in enumerate((es_h, em_h, ns_h, nm_h))
    ]
    loads = [pltpu.make_async_copy(a, b, in_sem.at[i]) for i, (a, b) in enumerate(staged)]

    barrier = pltpu.get_barrier_semaphore()

    def greet(to_lon, to_lat):
        pl.semaphore_signal(
            barrier, inc=1, device_id={"lon": to_lon, "lat": to_lat}, device_id_type=MESH
        )

    greet(east, lat)
    greet(west, lat)
    greet(up_main, north)

    @pl.when(not_self_east)
    def _():
        greet(up_east, north)

    @pl.when(not_self_west)
    def _():
        greet(up_west, north)

    @pl.when(not_bottom)
    def _():
        greet(lon, south)
        greet(east, south)
        greet(west, south)

    for c in loads:
        c.start()

    lane = lax.broadcasted_iota(jnp.int32, (8, LANES), 1)
    sub = lax.broadcasted_iota(jnp.int32, (8, LANES), 0)

    def roll(x, shift):
        return pltpu.roll(x, shift % LANES, 1)

    def permute(x, source):
        return jnp.take_along_axis(x, source, axis=1)

    def exchange(tile):
        for bit in (1, 2, 4):
            keep = (lane & bit) == 0
            new = list(tile)
            for t in range(tiles):
                if not t & bit:
                    x, y = tile[t], tile[t + bit]
                    crossing = permute(jnp.where(keep, y, x), lane ^ bit)
                    new[t] = jnp.where(keep, x, crossing)
                    new[t + bit] = jnp.where(keep, crossing, y)
            tile = new
        return tile

    def lay_out(tile, target, end, r):
        rows = slice(PAD + 8 * r, PAD + 8 * r + 8)
        both = jnp.where(lane < LANES // 2, roll(tile[0], HALO), roll(tile[-1], -HALO))
        target[tiles, rows, :] = both
        end[8 * r : 8 * r + 8, :] = both
        for t, x in enumerate(exchange(tile)):
            target[t, rows, :] = x

    def block(r, t):
        return slice(8 * r, 8 * r + 8), slice(t * LANES, (t + 1) * LANES)

    def lay_state(lv):
        @pl.loop(0, 2)
        def _(kind):
            for r in range(row_tiles):
                wet = [mask_v[block(r, t)].astype(jnp.float32) for t in range(tiles)]
                for tr in range(2):
                    lay_out(
                        [state_v[kind, tr, lv, *block(r, t)] * wet[t] for t in range(tiles)],
                        state.at[0, lv, kind, tr],
                        ends.at[lv, 2 * kind + tr],
                        r,
                    )

    def lay_coef(lv):
        @pl.loop(0, 2)
        def _(pair):
            for j in range(2):
                for r in range(row_tiles):
                    lay_out(
                        [coef_v[2 * pair + j, lv, *block(r, t)] * SCALES[j] for t in range(tiles)],
                        coef.at[lv, 2 * pair + j],
                        ends.at[lv, 4 + 2 * pair + j],
                        r,
                    )

    slot_of_lane = lane // SLOT
    sign = jnp.where(is_top, -1.0, 1.0)

    def pack_ends(lv):
        for r in range(row_tiles):
            rows = slice(8 * r, 8 * r + 8)
            up = jnp.zeros((8, LANES), jnp.float32)
            down = jnp.zeros((8, LANES), jnp.float32)
            for s in range(8):
                here = slot_of_lane == s
                mine = ends[lv, s, rows, :]
                shift = (SLOT * s - (LANES - HALO - SLOT)) % LANES
                high = pltpu.roll(mine, shift + top, 1) if s in (4 + NS, 4 + NM) else roll(mine, shift)
                if s in (4 + ES, 4 + NS):
                    high = high * sign
                up = jnp.where(here, high, up)
                down = jnp.where(here, roll(mine, SLOT * s - HALO), down)
            pack[0, lv, rows, :] = up
            pack[1, lv, rows, :] = down

        @pl.when(is_top)
        def _():
            turned = []
            for r in range(row_tiles):
                x = permute(pack[0, lv, 8 * r : 8 * r + 8, :], lane ^ (SLOT - 1))
                for bit in (1, 2, 4):
                    x = jnp.where(
                        (sub & bit) == 0, pltpu.roll(x, 8 - bit, 0), pltpu.roll(x, bit, 0)
                    )
                turned.append(x)
            for r in range(row_tiles):
                pack[0, lv, 8 * r : 8 * r + 8, :] = turned[row_tiles - 1 - r]

    @pl.when(is_bottom)
    def _():
        land[0] = jnp.zeros(land.shape[1:], jnp.float32)

    def wait_peers():
        peers = 8 - jnp.where(is_bottom, 3, 0) - jnp.where(self_east, 1, 0) - jnp.where(self_west, 1, 0)
        pl.semaphore_wait(barrier, peers)

    own_rows = pl.ds(0, columns)
    last_rows, first_rows = pl.ds(columns - HALO, HALO), pl.ds(0, HALO)
    west_rows, east_rows = pl.ds(PAD - HALO, HALO), pl.ds(PAD + columns, HALO)

    def lat_copy(lv, out, src_rows, side, dst_rows, slot, to_lon, to_lat):
        return pltpu.make_async_remote_copy(
            src_ref=pack.at[out, lv, src_rows, :],
            dst_ref=land.at[side, lv, dst_rows, :],
            send_sem=lat_send.at[out, lv, slot],
            recv_sem=lat_recv.at[side, lv, slot],
            device_id={"lon": to_lon, "lat": to_lat},
            device_id_type=MESH,
        )

    def up_copies(lv):
        return [
            lat_copy(lv, 0, own_rows, top, own, 0, up_main, north),
            lat_copy(lv, 0, last_rows, top, west_rows, 1, up_east, north),
            lat_copy(lv, 0, first_rows, top, east_rows, 2, up_west, north),
        ]

    def down_copies(lv):
        return [
            lat_copy(lv, 1, own_rows, 1, own, 0, lon, south),
            lat_copy(lv, 1, last_rows, 1, west_rows, 1, east, south),
            lat_copy(lv, 1, first_rows, 1, east_rows, 2, west, south),
        ]

    def self_copies(lv):
        return [
            pltpu.make_async_copy(
                pack.at[0, lv, last_rows, :], land.at[1, lv, west_rows, :], self_sem.at[lv, 0]
            ),
            pltpu.make_async_copy(
                pack.at[0, lv, first_rows, :], land.at[1, lv, east_rows, :], self_sem.at[lv, 1]
            ),
        ]

    def each_way(to_main, to_east, to_west, own_east, own_west, to_south):
        to_main()
        pl.when(not_self_east)(to_east)
        pl.when(not_self_west)(to_west)
        pl.when(self_east)(own_east)
        pl.when(self_west)(own_west)
        pl.when(not_bottom)(to_south)

    def send_lat(lv):
        ups, downs, selves = up_copies(lv), down_copies(lv), self_copies(lv)

        def to_south():
            for c in downs:
                c.start()

        each_way(ups[0].start, ups[1].start, ups[2].start, selves[0].start, selves[1].start, to_south)

    def lat_in(lv):
        norths, selves = down_copies(lv), self_copies(lv)

        def from_south():
            for slot, (src, dst) in enumerate(
                ((own_rows, own), (last_rows, west_rows), (first_rows, east_rows))
            ):
                lat_copy(lv, 0, src, 0, dst, slot, lon, lat).wait_recv()

        each_way(
            norths[0].wait_recv, norths[1].wait_recv, norths[2].wait_recv,
            selves[0].wait, selves[1].wait, from_south,
        )

    def lat_sent(lv):
        ups, downs = up_copies(lv), down_copies(lv)

        def to_south():
            for c in downs:
                c.wait_send()

        def nothing():
            pass

        each_way(ups[0].wait_send, ups[1].wait_send, ups[2].wait_send, nothing, nothing, to_south)

    def lon_copies(way, lv, to_lon):
        main_tiles = pl.ds(0, tiles)

        def part(source, first, target, width, skip=0):
            begin = first + (columns - skip - width if way == 0 else skip)
            dst = PAD - skip - width if way == 0 else PAD + columns + skip
            return source.at[..., pl.ds(begin, width), :], target.at[..., pl.ds(dst, width), :]

        def main_part(ref, width, skip=0):
            return part(ref, PAD, ref, width, skip)

        parts = [
            main_part(state.at[k, lv, kind, :, main_tiles], width, 2 * k)
            for k in range(3)
            for kind, width in ((NEW, 4), (OLD, 3))
        ] + [
            main_part(coef.at[lv, pl.ds(ES, 2), main_tiles], 7 if way == 0 else 6),
            main_part(coef.at[lv, pl.ds(NS, 2), main_tiles], 6),
            part(ends.at[lv, pl.ds(0, 2)], 0, state.at[0, lv, OLD, :, tiles], HALO),
            part(ends.at[lv, pl.ds(2, 2)], 0, state.at[0, lv, NEW, :, tiles], HALO),
            part(ends.at[lv, pl.ds(4, 4)], 0, coef.at[lv, :, tiles], HALO),
        ]
        return [
            pltpu.make_async_remote_copy(
                src_ref=src,
                dst_ref=dst,
                send_sem=lon_send.at[way, lv, i],
                recv_sem=lon_recv.at[way, lv, i],
                device_id={"lon": to_lon, "lat": lat},
                device_id_type=MESH,
            )
            for i, (src, dst) in enumerate(parts)
        ]

    def send_lon(lv, parts):
        a, b = lon_copies(0, lv, east), lon_copies(1, lv, west)
        for i in parts:
            a[i].start()
            b[i].start()

    AT_ONCE, STEPPED = (0, 1, 8, 9, 6, 7, 10), (2, 3, 4, 5)

    next_lane = jnp.where(lane >= LANES - 8, lane - (LANES - 9), lane + 8)
    last_lane = jnp.where(lane < 8, lane + (LANES - 9), lane - 8)

    def after(x):
        return [roll(x[0], -1)] if len(x) == 1 else x[1:] + [permute(x[0], next_lane)]

    def before(x):
        return [roll(x[0], 1)] if len(x) == 1 else [permute(x[-1], last_lane)] + x[:-1]

    def eastern(x):
        y = [pltpu.roll(a, 7, 0) for a in x]
        return [jnp.where(sub == 7, b, a) for a, b in zip(y, y[1:])] + y[-1:]

    def western(x):
        y = [pltpu.roll(a, 1, 0) for a in x]
        return y[:1] + [jnp.where(sub == 0, a, b) for a, b in zip(y, y[1:])]

    def advance(k, lv, slot, base, count, group):
        frames = [pl.ds(base + 8 * i, 8) for i in range(count)]
        old = state.at[k - 1, lv]
        for t in group:
            es = [coef[lv, ES, t, rows, :] for rows in frames]
            em = [coef[lv, EM, t, rows, :] for rows in frames]
            for tr in range(2):
                n = [old[NEW, tr, t, rows, :] for rows in frames]
                o = [old[OLD, tr, t, rows, :] for rows in frames]
                near = [a + b for a, b in zip(n, eastern(n))]
                flow = [
                    u * (8.0 * here - (a + b)) - v * (o1 - o0)
                    for u, v, here, a, b, o1, o0 in zip(
                        es, em, near, eastern(near), western(near), eastern(o), o
                    )
                ]
                for i, (a, b) in enumerate(zip(flow, western(flow))):
                    div[slot, tr, t, 8 * i : 8 * i + 8, :] = a - b
        for i, rows in enumerate(frames):
            mine = slice(8 * i, 8 * i + 8)
            for tr in range(2):
                n = [old[NEW, tr, t, rows, :] for t in group]
                o = [old[OLD, tr, t, rows, :] for t in group]
                near = [a + b for a, b in zip(n, after(n))]
                flow = [
                    coef[lv, NS, t, rows, :] * (8.0 * here - (a + b)) - coef[lv, NM, t, rows, :] * (o1 - o0)
                    for t, here, a, b, o1, o0 in zip(
                        group, near, after(near), before(near), after(o), o
                    )
                ]
                for j, (t, a, b) in enumerate(zip(group, flow, before(flow))):
                    fresh = o[j] - (div[slot, tr, t, mine, :] + (a - b))
                    held[slot, NEW, tr, t, mine, :] = fresh
                    held[slot, OLD, tr, t, mine, :] = (1.0 - 2.0 * GAMMA) * n[j] + GAMMA * (
                        o[j] + fresh
                    )

    def keep(k, lv, slot, base, windows, group):
        for kind in (NEW, OLD):
            for tr in range(2):
                for t in group:
                    for w in windows:
                        state[k, lv, kind, tr, t, pl.ds(base + w, 8), :] = held[
                            slot, kind, tr, t, w : w + 8, :
                        ]

    main, edge = list(range(tiles)), [tiles]

    def inner_place(u):
        k = jnp.where(u < 3, 1, jnp.where(u > 9, 6, (u - 3) // 2 + 2))
        j = jnp.where(u < 3, u, jnp.where(u < 9, lax.rem(u - 3, 2), 0))
        gap = jnp.where(u < 3, 8, 20 - 4 * k)
        return k, PAD + jnp.minimum(2 * k, 10) + j * gap

    def inner_unit(u, levels):
        k, r0 = inner_place(u)
        for slot, lv in enumerate(levels):
            advance(k, lv, slot, r0 - 2, 2, main)
        for slot, lv in enumerate(levels):
            keep(k, lv, slot, r0 - 2, (2, 6), main)

    place = lax.rem(lon, n_lon // 2)
    patient = jnp.logical_or(place == 0, jnp.logical_and(is_top, place < n_lon // 4))
    for c in loads[:3]:
        c.wait()

    @pl.loop(0, 2)
    def _(lv):
        lay_state(lv)

        @pl.when(jnp.logical_not(patient))
        def _():
            @pl.when(lv == 0)
            def _():
                wait_peers()

            send_lon(lv, AT_ONCE[:4])

        @pl.when(lv == 0)
        def _():
            for c in loads[3:]:
                c.wait()

        lay_coef(lv)

        @pl.when(jnp.logical_not(patient))
        def _():
            send_lon(lv, AT_ONCE[4:])

        pack_ends(lv)

        @pl.when(jnp.logical_not(patient))
        def _():
            send_lat(lv)

        @pl.loop(0, FIRST)
        def _(u):
            inner_unit(u, [lv])

        @pl.when(jnp.logical_not(patient))
        def _():
            send_lon(lv, STEPPED)

    @pl.when(patient)
    def _():
        wait_peers()

        @pl.loop(0, 2)
        def _(lv):
            send_lat(lv)
            send_lon(lv, AT_ONCE + STEPPED)

    @pl.loop(FIRST, 11)
    def _(u):
        inner_unit(u, range(2))

    even = lax.rem(lon, 2) == 0
    outs = (lag_h, lat_h)
    wide = range((columns + 2 * HALO) // 8)

    def side_in(do_east, lv):
        @pl.when(do_east)
        def _():
            for c in lon_copies(1, lv, west):
                c.wait_recv()
            for c in lon_copies(0, lv, east):
                c.wait_send()

        @pl.when(jnp.logical_not(do_east))
        def _():
            for c in lon_copies(0, lv, east):
                c.wait_recv()
            for c in lon_copies(1, lv, west):
                c.wait_send()

    def side_base(do_east, k):
        west_base = jnp.maximum(2 * k - UNIT, -2 * k)
        return jnp.where(do_east, PAD + columns - UNIT - west_base, PAD + west_base) - 2

    def finish(do_east, lv):
        first = pl.multiple_of(jnp.where(do_east, columns // 2, 0), 16)

        for kind in (OLD, NEW):
            for r in range(2):
                rows = pl.ds(pl.multiple_of(first + 8 * r, 8), 8)
                source = pl.ds(pl.multiple_of(PAD + first + 8 * r, 8), 8)
                for tr in range(2):
                    tile = exchange([state[STEPS, lv, kind, tr, t, source, :] for t in main])
                    for t in main:
                        state_v[kind, tr, lv, rows, t * LANES : (t + 1) * LANES] = tile[t]

    @pl.loop(0, 2)
    def _(lv):
        side_in(even, lv)

        @pl.loop(1, STEPS + 1)
        def _(k):
            base = side_base(even, k)
            advance(k, lv, 0, base, 2, main)
            keep(k, lv, 0, base, (2, 6), main)

        finish(even, lv)

    def unpack(lv, begins):
        done = []
        for begin in begins:
            rows = pl.ds(begin, 8)
            for f in range(8):
                source = pl.ds(begin + top, 8) if f in (4 + ES, 4 + EM) else rows
                north_part = roll(land[1, lv, source, :], LANES - HALO - SLOT * f)
                south_part = roll(land[0, lv, rows, :], HALO - SLOT - SLOT * f)
                if f < 4:
                    target = state.at[0, lv, f // 2, f % 2, tiles]
                else:
                    target = coef.at[lv, f - 4, tiles]
                inside = jnp.where(lane < HALO, south_part, target[rows, :])
                done.append((target, rows, jnp.where(lane >= LANES - HALO, north_part, inside)))
        for target, rows, value in done:
            target[rows, :] = value

    @pl.loop(0, 2)
    def _(lv):
        do_east = jnp.logical_not(even)
        lat_in(lv)
        side_in(do_east, lv)
        unpack(lv, [PAD - HALO + 8 * r for r in wide])

        @pl.loop(1, STEPS + 1)
        def _(k):
            base = side_base(do_east, k)
            advance(k, lv, 0, base, 2, main)
            advance(k, lv, 0, PAD - HALO, len(wide), edge)
            keep(k, lv, 0, base, (2, 6), main)
            keep(k, lv, 0, PAD - HALO, [8 * r for r in wide], edge)

        finish(do_east, lv)
        for kind in (OLD, NEW):
            for tr in range(2):
                for r in range(row_tiles):
                    rows = slice(8 * r, 8 * r + 8)
                    end = state[STEPS, lv, kind, tr, tiles, PAD + 8 * r : PAD + 8 * r + 8, :]
                    for t in main:
                        here = state_v[kind, tr, lv, rows, t * LANES : (t + 1) * LANES]
                        if t == 0:
                            here = jnp.where(lane < HALO, roll(end, -HALO), here)
                        if t == tiles - 1:
                            here = jnp.where(lane >= LANES - HALO, roll(end, HALO), here)
                        outs[kind][tr, lv, rows, t * LANES : (t + 1) * LANES] = here

    @pl.loop(0, 2)
    def _(lv):
        lat_sent(lv)


def solution(mesh):
    n_lon, n_lat = mesh.shape["lon"], mesh.shape["lat"]

    def shards(previous, current, east_speed, north_speed, east_mix, north_mix, sea_mask):
        columns, height = previous.shape[2:]
        tiles = height // LANES
        rows = columns + 2 * PAD
        field = jax.ShapeDtypeStruct(previous.shape, jnp.float32)
        f32 = jnp.float32
        done = pl.pallas_call(
            functools.partial(kernel, (n_lon, n_lat, columns, height)),
            out_shape=(pltpu.VMEM(previous.shape, f32), pltpu.VMEM(previous.shape, f32)),
            in_specs=[pl.BlockSpec(memory_space=pl.ANY)] * 7,
            out_specs=[pl.BlockSpec(memory_space=pltpu.VMEM)] * 2,
            scratch_shapes=[
                pltpu.VMEM(sea_mask.shape, sea_mask.dtype),
                pltpu.VMEM((2, *previous.shape), f32),
                pltpu.VMEM((4, *east_speed.shape), f32),
                pltpu.VMEM((STEPS + 1, 2, 2, 2, tiles + 1, rows, LANES), f32),
                pltpu.VMEM((2, 4, tiles + 1, rows, LANES), f32),
                pltpu.VMEM((2, 8, columns, LANES), f32),
                pltpu.VMEM((2, 2, tiles + 1, rows, LANES), f32),
                pltpu.VMEM((2, 2, 2, tiles + 1, rows, LANES), f32),
                pltpu.VMEM((2, 2, columns, LANES), f32),
                pltpu.VMEM((2, 2, rows, LANES), f32),
                pltpu.SemaphoreType.DMA((7,)),
                pltpu.SemaphoreType.DMA((2, 2, 11)),
                pltpu.SemaphoreType.DMA((2, 2, 11)),
                pltpu.SemaphoreType.DMA((2, 2, 3)),
                pltpu.SemaphoreType.DMA((2, 2, 3)),
                pltpu.SemaphoreType.DMA((2, 2)),
            ],
            compiler_params=pltpu.CompilerParams(
                collective_id=0, has_side_effects=True, vmem_limit_bytes=60 * 2**20
            ),
            cost_estimate=pl.CostEstimate(
                flops=30 * STEPS * previous.size, bytes_accessed=16 * previous.size, transcendentals=0
            ),
        )(previous, current, east_speed, north_speed, east_mix, north_mix, sea_mask)
        def hand_over(a, b, x, y, sems):
            copies = [
                pltpu.make_async_copy(src.at[tr], dst.at[tr], sems.at[i, tr])
                for i, (src, dst) in enumerate(((a, x), (b, y)))
                for tr in range(2)
            ]
            for c in copies:
                c.start()
            for c in copies:
                c.wait()

        return pl.pallas_call(
            hand_over,
            out_shape=(field, field),
            in_specs=[pl.BlockSpec(memory_space=pl.ANY)] * 2,
            out_specs=[pl.BlockSpec(memory_space=pl.ANY)] * 2,
            scratch_shapes=[pltpu.SemaphoreType.DMA((2, 2))],
            name="hand_over",
            compiler_params=pltpu.CompilerParams(vmem_limit_bytes=2**20),
        )(*done)


    return jax.shard_map(
        shards,
        mesh=mesh,
        in_specs=(
            P(None, None, "lon", "lat"),
            P(None, None, "lon", "lat"),
            P(None, "lon", "lat"),
            P(None, "lon", "lat"),
            P(None, "lon", "lat"),
            P(None, "lon", "lat"),
            P("lon", "lat"),
        ),
        out_specs=(P(None, None, "lon", "lat"), P(None, None, "lon", "lat")),
        check_vma=False,
    )
```

```python
import functools

import jax
import jax.numpy as jnp
from jax import lax
from jax.experimental import pallas as pl
from jax.experimental.pallas import tpu as pltpu
from jax.sharding import PartitionSpec as P

STEPS = 6
GAMMA = 0.1
MESH = pl.DeviceIdType.MESH

LANES = 128
PAD = 16
HALO = 2 * STEPS
SLOT = 16
UNIT = HALO
FIRST = 5
OLD, NEW = 0, 1
ES, EM, NS, NM = range(4)
SCALES = (2.0 / 12.0, 2.0)


def kernel(sizes, *refs):
    n_lon, n_lat, columns, height = sizes
    (prev_h, cur_h, es_h, ns_h, em_h, nm_h, mask_h, lag_h, lat_h) = refs[:9]
    (mask_v, state_v, coef_v, state, coef, ends, div, held, pack, land) = refs[9:19]
    (in_sem, lon_send, lon_recv, lat_send, lat_recv, self_sem) = refs[19:]
    tiles = height // LANES
    ring = tiles + 1
    row_tiles = columns // 8
    own = pl.ds(PAD, columns)

    lon, lat = lax.axis_index("lon"), lax.axis_index("lat")
    east, west = lax.rem(lon + 1, n_lon), lax.rem(lon + n_lon - 1, n_lon)
    is_top, is_bottom = lat == n_lat - 1, lat == 0
    top = jnp.where(is_top, 1, 0)
    north, south = jnp.minimum(lat + 1, n_lat - 1), jnp.maximum(lat - 1, 0)
    up_main = jnp.where(is_top, n_lon - 1 - lon, lon)
    up_east = jnp.where(is_top, lax.rem(n_lon - lon, n_lon), east)
    up_west = jnp.where(is_top, lax.rem(2 * n_lon - 2 - lon, n_lon), west)
    self_east = jnp.logical_and(is_top, up_east == lon)
    self_west = jnp.logical_and(is_top, up_west == lon)
    not_self_east = jnp.logical_not(self_east)
    not_self_west = jnp.logical_not(self_west)
    not_bottom = jnp.logical_not(is_bottom)

    staged = [(mask_h, mask_v), (cur_h, state_v.at[NEW]), (prev_h, state_v.at[OLD])] + [
        (ref, coef_v.at[field]) for field, ref in enumerate((es_h, em_h, ns_h, nm_h))
    ]
    loads = [pltpu.make_async_copy(a, b, in_sem.at[i]) for i, (a, b) in enumerate(staged)]

    barrier = pltpu.get_barrier_semaphore()

    def greet(to_lon, to_lat):
        pl.semaphore_signal(
            barrier, inc=1, device_id={"lon": to_lon, "lat": to_lat}, device_id_type=MESH
        )

    greet(east, lat)
    greet(west, lat)
    greet(up_main, north)

    @pl.when(not_self_east)
    def _():
        greet(up_east, north)

    @pl.when(not_self_west)
    def _():
        greet(up_west, north)

    @pl.when(not_bottom)
    def _():
        greet(lon, south)
        greet(east, south)
        greet(west, south)

    for c in loads:
        c.start()

    lane = lax.broadcasted_iota(jnp.int32, (8, LANES), 1)
    sub = lax.broadcasted_iota(jnp.int32, (8, LANES), 0)

    def roll(x, shift):
        return pltpu.roll(x, shift % LANES, 1)

    def permute(x, source):
        return jnp.take_along_axis(x, source, axis=1)

    def exchange(tile):
        for bit in (1, 2, 4):
            keep = (lane & bit) == 0
            new = list(tile)
            for t in range(tiles):
                if not t & bit:
                    x, y = tile[t], tile[t + bit]
                    crossing = permute(jnp.where(keep, y, x), lane ^ bit)
                    new[t] = jnp.where(keep, x, crossing)
                    new[t + bit] = jnp.where(keep, crossing, y)
            tile = new
        return tile

    def lay_out(tile, target, end, r):
        rows = slice(PAD + 8 * r, PAD + 8 * r + 8)
        both = jnp.where(lane < LANES // 2, roll(tile[0], HALO), roll(tile[-1], -HALO))
        target[tiles, rows, :] = both
        end[8 * r : 8 * r + 8, :] = both
        for t, x in enumerate(exchange(tile)):
            target[t, rows, :] = x

    def block(r, t):
        return slice(8 * r, 8 * r + 8), slice(t * LANES, (t + 1) * LANES)

    def lay_state(lv):
        @pl.loop(0, 2)
        def _(kind):
            for r in range(row_tiles):
                wet = [mask_v[block(r, t)].astype(jnp.float32) for t in range(tiles)]
                for tr in range(2):
                    lay_out(
                        [state_v[kind, tr, lv, *block(r, t)] * wet[t] for t in range(tiles)],
                        state.at[0, lv, kind, tr],
                        ends.at[lv, 2 * kind + tr],
                        r,
                    )

    def lay_coef(lv):
        @pl.loop(0, 2)
        def _(pair):
            for j in range(2):
                for r in range(row_tiles):
                    lay_out(
                        [coef_v[2 * pair + j, lv, *block(r, t)] * SCALES[j] for t in range(tiles)],
                        coef.at[lv, 2 * pair + j],
                        ends.at[lv, 4 + 2 * pair + j],
                        r,
                    )

    slot_of_lane = lane // SLOT
    sign = jnp.where(is_top, -1.0, 1.0)

    def pack_ends(lv):
        for r in range(row_tiles):
            rows = slice(8 * r, 8 * r + 8)
            up = jnp.zeros((8, LANES), jnp.float32)
            down = jnp.zeros((8, LANES), jnp.float32)
            for s in range(8):
                here = slot_of_lane == s
                mine = ends[lv, s, rows, :]
                shift = (SLOT * s - (LANES - HALO - SLOT)) % LANES
                high = pltpu.roll(mine, shift + top, 1) if s in (4 + NS, 4 + NM) else roll(mine, shift)
                if s in (4 + ES, 4 + NS):
                    high = high * sign
                up = jnp.where(here, high, up)
                down = jnp.where(here, roll(mine, SLOT * s - HALO), down)
            pack[0, lv, rows, :] = up
            pack[1, lv, rows, :] = down

        @pl.when(is_top)
        def _():
            turned = []
            for r in range(row_tiles):
                x = permute(pack[0, lv, 8 * r : 8 * r + 8, :], lane ^ (SLOT - 1))
                for bit in (1, 2, 4):
                    x = jnp.where(
                        (sub & bit) == 0, pltpu.roll(x, 8 - bit, 0), pltpu.roll(x, bit, 0)
                    )
                turned.append(x)
            for r in range(row_tiles):
                pack[0, lv, 8 * r : 8 * r + 8, :] = turned[row_tiles - 1 - r]

    @pl.when(is_bottom)
    def _():
        land[0] = jnp.zeros(land.shape[1:], jnp.float32)

    def wait_peers():
        peers = 8 - jnp.where(is_bottom, 3, 0) - jnp.where(self_east, 1, 0) - jnp.where(self_west, 1, 0)
        pl.semaphore_wait(barrier, peers)

    own_rows = pl.ds(0, columns)
    last_rows, first_rows = pl.ds(columns - HALO, HALO), pl.ds(0, HALO)
    west_rows, east_rows = pl.ds(PAD - HALO, HALO), pl.ds(PAD + columns, HALO)

    def lat_copy(lv, out, src_rows, side, dst_rows, slot, to_lon, to_lat):
        return pltpu.make_async_remote_copy(
            src_ref=pack.at[out, lv, src_rows, :],
            dst_ref=land.at[side, lv, dst_rows, :],
            send_sem=lat_send.at[out, lv, slot],
            recv_sem=lat_recv.at[side, lv, slot],
            device_id={"lon": to_lon, "lat": to_lat},
            device_id_type=MESH,
        )

    def up_copies(lv):
        return [
            lat_copy(lv, 0, own_rows, top, own, 0, up_main, north),
            lat_copy(lv, 0, last_rows, top, west_rows, 1, up_east, north),
            lat_copy(lv, 0, first_rows, top, east_rows, 2, up_west, north),
        ]

    def down_copies(lv):
        return [
            lat_copy(lv, 1, own_rows, 1, own, 0, lon, south),
            lat_copy(lv, 1, last_rows, 1, west_rows, 1, east, south),
            lat_copy(lv, 1, first_rows, 1, east_rows, 2, west, south),
        ]

    def self_copies(lv):
        return [
            pltpu.make_async_copy(
                pack.at[0, lv, last_rows, :], land.at[1, lv, west_rows, :], self_sem.at[lv, 0]
            ),
            pltpu.make_async_copy(
                pack.at[0, lv, first_rows, :], land.at[1, lv, east_rows, :], self_sem.at[lv, 1]
            ),
        ]

    def each_way(to_main, to_east, to_west, own_east, own_west, to_south):
        to_main()
        pl.when(not_self_east)(to_east)
        pl.when(not_self_west)(to_west)
        pl.when(self_east)(own_east)
        pl.when(self_west)(own_west)
        pl.when(not_bottom)(to_south)

    def send_lat(lv):
        ups, downs, selves = up_copies(lv), down_copies(lv), self_copies(lv)

        def to_south():
            for c in downs:
                c.start()

        each_way(ups[0].start, ups[1].start, ups[2].start, selves[0].start, selves[1].start, to_south)

    def lat_in(lv):
        norths, selves = down_copies(lv), self_copies(lv)

        def from_south():
            for slot, (src, dst) in enumerate(
                ((own_rows, own), (last_rows, west_rows), (first_rows, east_rows))
            ):
                lat_copy(lv, 0, src, 0, dst, slot, lon, lat).wait_recv()

        each_way(
            norths[0].wait_recv, norths[1].wait_recv, norths[2].wait_recv,
            selves[0].wait, selves[1].wait, from_south,
        )

    def lat_sent(lv):
        ups, downs = up_copies(lv), down_copies(lv)

        def to_south():
            for c in downs:
                c.wait_send()

        def nothing():
            pass

        each_way(ups[0].wait_send, ups[1].wait_send, ups[2].wait_send, nothing, nothing, to_south)

    def lon_copies(way, lv, to_lon):
        main_tiles = pl.ds(0, tiles)

        def part(source, first, target, width, skip=0):
            begin = first + (columns - skip - width if way == 0 else skip)
            dst = PAD - skip - width if way == 0 else PAD + columns + skip
            return source.at[..., pl.ds(begin, width), :], target.at[..., pl.ds(dst, width), :]

        def main_part(ref, width, skip=0):
            return part(ref, PAD, ref, width, skip)

        parts = [
            main_part(state.at[k, lv, kind, :, main_tiles], width, 2 * k)
            for k in range(3)
            for kind, width in ((NEW, 4), (OLD, 3))
        ] + [
            main_part(coef.at[lv, pl.ds(ES, 2), main_tiles], 7 if way == 0 else 6),
            main_part(coef.at[lv, pl.ds(NS, 2), main_tiles], 6),
            part(ends.at[lv, pl.ds(0, 2)], 0, state.at[0, lv, OLD, :, tiles], HALO),
            part(ends.at[lv, pl.ds(2, 2)], 0, state.at[0, lv, NEW, :, tiles], HALO),
            part(ends.at[lv, pl.ds(4, 4)], 0, coef.at[lv, :, tiles], HALO),
        ]
        return [
            pltpu.make_async_remote_copy(
                src_ref=src,
                dst_ref=dst,
                send_sem=lon_send.at[way, lv, i],
                recv_sem=lon_recv.at[way, lv, i],
                device_id={"lon": to_lon, "lat": lat},
                device_id_type=MESH,
            )
            for i, (src, dst) in enumerate(parts)
        ]

    def send_lon(lv, parts):
        a, b = lon_copies(0, lv, east), lon_copies(1, lv, west)
        for i in parts:
            a[i].start()
            b[i].start()

    AT_ONCE, STEPPED = (0, 1, 8, 9, 6, 7, 10), (2, 3, 4, 5)

    next_lane = jnp.where(lane >= LANES - 8, lane - (LANES - 9), lane + 8)
    last_lane = jnp.where(lane < 8, lane + (LANES - 9), lane - 8)

    def after(x):
        return [roll(x[0], -1)] if len(x) == 1 else x[1:] + [permute(x[0], next_lane)]

    def before(x):
        return [roll(x[0], 1)] if len(x) == 1 else [permute(x[-1], last_lane)] + x[:-1]

    def eastern(x):
        y = [pltpu.roll(a, 7, 0) for a in x]
        return [jnp.where(sub == 7, b, a) for a, b in zip(y, y[1:])] + y[-1:]

    def western(x):
        y = [pltpu.roll(a, 1, 0) for a in x]
        return y[:1] + [jnp.where(sub == 0, a, b) for a, b in zip(y, y[1:])]

    def advance(k, lv, slot, base, count, group):
        frames = [pl.ds(base + 8 * i, 8) for i in range(count)]
        old = state.at[k - 1, lv]
        for t in group:
            es = [coef[lv, ES, t, rows, :] for rows in frames]
            em = [coef[lv, EM, t, rows, :] for rows in frames]
            for tr in range(2):
                n = [old[NEW, tr, t, rows, :] for rows in frames]
                o = [old[OLD, tr, t, rows, :] for rows in frames]
                near = [a + b for a, b in zip(n, eastern(n))]
                flow = [
                    u * (8.0 * here - (a + b)) - v * (o1 - o0)
                    for u, v, here, a, b, o1, o0 in zip(
                        es, em, near, eastern(near), western(near), eastern(o), o
                    )
                ]
                for i, (a, b) in enumerate(zip(flow, western(flow))):
                    div[slot, tr, t, 8 * i : 8 * i + 8, :] = a - b
        for i, rows in enumerate(frames):
            mine = slice(8 * i, 8 * i + 8)
            for tr in range(2):
                n = [old[NEW, tr, t, rows, :] for t in group]
                o = [old[OLD, tr, t, rows, :] for t in group]
                near = [a + b for a, b in zip(n, after(n))]
                flow = [
                    coef[lv, NS, t, rows, :] * (8.0 * here - (a + b)) - coef[lv, NM, t, rows, :] * (o1 - o0)
                    for t, here, a, b, o1, o0 in zip(
                        group, near, after(near), before(near), after(o), o
                    )
                ]
                for j, (t, a, b) in enumerate(zip(group, flow, before(flow))):
                    fresh = o[j] - (div[slot, tr, t, mine, :] + (a - b))
                    held[slot, NEW, tr, t, mine, :] = fresh
                    held[slot, OLD, tr, t, mine, :] = (1.0 - 2.0 * GAMMA) * n[j] + GAMMA * (
                        o[j] + fresh
                    )

    def keep(k, lv, slot, base, windows, group):
        for kind in (NEW, OLD):
            for tr in range(2):
                for t in group:
                    for w in windows:
                        state[k, lv, kind, tr, t, pl.ds(base + w, 8), :] = held[
                            slot, kind, tr, t, w : w + 8, :
                        ]

    main, edge = list(range(tiles)), [tiles]

    def inner_place(u):
        k = jnp.where(u < 3, 1, jnp.where(u > 9, 6, (u - 3) // 2 + 2))
        j = jnp.where(u < 3, u, jnp.where(u < 9, lax.rem(u - 3, 2), 0))
        gap = jnp.where(u < 3, 8, 20 - 4 * k)
        return k, PAD + jnp.minimum(2 * k, 10) + j * gap

    def inner_unit(u, levels):
        k, r0 = inner_place(u)
        for slot, lv in enumerate(levels):
            advance(k, lv, slot, r0 - 2, 2, main)
        for slot, lv in enumerate(levels):
            keep(k, lv, slot, r0 - 2, (2, 6), main)

    place = lax.rem(lon, n_lon // 2)
    patient = jnp.logical_or(place == 0, jnp.logical_and(is_top, place < n_lon // 4))
    for c in loads[:3]:
        c.wait()

    @pl.loop(0, 2)
    def _(lv):
        lay_state(lv)

        @pl.when(jnp.logical_not(patient))
        def _():
            @pl.when(lv == 0)
            def _():
                wait_peers()

            send_lon(lv, AT_ONCE[:4])

        @pl.when(lv == 0)
        def _():
            for c in loads[3:]:
                c.wait()

        lay_coef(lv)

        @pl.when(jnp.logical_not(patient))
        def _():
            send_lon(lv, AT_ONCE[4:])

        pack_ends(lv)

        @pl.when(jnp.logical_not(patient))
        def _():
            send_lat(lv)

        @pl.loop(0, FIRST)
        def _(u):
            inner_unit(u, [lv])

        @pl.when(jnp.logical_not(patient))
        def _():
            send_lon(lv, STEPPED)

    @pl.when(patient)
    def _():
        wait_peers()

        @pl.loop(0, 2)
        def _(lv):
            send_lat(lv)
            send_lon(lv, AT_ONCE + STEPPED)

    @pl.loop(FIRST, 11)
    def _(u):
        inner_unit(u, range(2))

    even = lax.rem(lon, 2) == 0
    outs = (lag_h, lat_h)
    wide = range((columns + 2 * HALO) // 8)

    def side_in(do_east, lv):
        @pl.when(do_east)
        def _():
            for c in lon_copies(1, lv, west):
                c.wait_recv()
            for c in lon_copies(0, lv, east):
                c.wait_send()

        @pl.when(jnp.logical_not(do_east))
        def _():
            for c in lon_copies(0, lv, east):
                c.wait_recv()
            for c in lon_copies(1, lv, west):
                c.wait_send()

    def side_base(do_east, k):
        west_base = jnp.maximum(2 * k - UNIT, -2 * k)
        return jnp.where(do_east, PAD + columns - UNIT - west_base, PAD + west_base) - 2

    def finish(do_east, lv):
        first = pl.multiple_of(jnp.where(do_east, columns // 2, 0), 16)

        for kind in (OLD, NEW):
            for r in range(2):
                rows = pl.ds(pl.multiple_of(first + 8 * r, 8), 8)
                source = pl.ds(pl.multiple_of(PAD + first + 8 * r, 8), 8)
                for tr in range(2):
                    tile = exchange([state[STEPS, lv, kind, tr, t, source, :] for t in main])
                    for t in main:
                        outs[kind][tr, lv, rows, t * LANES : (t + 1) * LANES] = tile[t]

    @pl.loop(0, 2)
    def _(lv):
        side_in(even, lv)

        @pl.loop(1, STEPS + 1)
        def _(k):
            base = side_base(even, k)
            advance(k, lv, 0, base, 2, main)
            keep(k, lv, 0, base, (2, 6), main)

        finish(even, lv)

    def unpack(lv, begins):
        done = []
        for begin in begins:
            rows = pl.ds(begin, 8)
            for f in range(8):
                source = pl.ds(begin + top, 8) if f in (4 + ES, 4 + EM) else rows
                north_part = roll(land[1, lv, source, :], LANES - HALO - SLOT * f)
                south_part = roll(land[0, lv, rows, :], HALO - SLOT - SLOT * f)
                if f < 4:
                    target = state.at[0, lv, f // 2, f % 2, tiles]
                else:
                    target = coef.at[lv, f - 4, tiles]
                inside = jnp.where(lane < HALO, south_part, target[rows, :])
                done.append((target, rows, jnp.where(lane >= LANES - HALO, north_part, inside)))
        for target, rows, value in done:
            target[rows, :] = value

    @pl.loop(0, 2)
    def _(lv):
        do_east = jnp.logical_not(even)
        lat_in(lv)
        side_in(do_east, lv)
        unpack(lv, [PAD - HALO + 8 * r for r in wide])

        @pl.loop(1, STEPS + 1)
        def _(k):
            base = side_base(do_east, k)
            advance(k, lv, 0, base, 2, main)
            advance(k, lv, 0, PAD - HALO, len(wide), edge)
            keep(k, lv, 0, base, (2, 6), main)
            keep(k, lv, 0, PAD - HALO, [8 * r for r in wide], edge)

        finish(do_east, lv)
        for kind in (OLD, NEW):
            for tr in range(2):
                for r in range(row_tiles):
                    rows = slice(8 * r, 8 * r + 8)
                    end = state[STEPS, lv, kind, tr, tiles, PAD + 8 * r : PAD + 8 * r + 8, :]
                    for t in (0, tiles - 1):
                        here = outs[kind][tr, lv, rows, t * LANES : (t + 1) * LANES]
                        if t == 0:
                            here = jnp.where(lane < HALO, roll(end, -HALO), here)
                        if t == tiles - 1:
                            here = jnp.where(lane >= LANES - HALO, roll(end, HALO), here)
                        outs[kind][tr, lv, rows, t * LANES : (t + 1) * LANES] = here

    @pl.loop(0, 2)
    def _(lv):
        lat_sent(lv)


def solution(mesh):
    n_lon, n_lat = mesh.shape["lon"], mesh.shape["lat"]

    def shards(previous, current, east_speed, north_speed, east_mix, north_mix, sea_mask):
        columns, height = previous.shape[2:]
        tiles = height // LANES
        rows = columns + 2 * PAD
        field = jax.ShapeDtypeStruct(previous.shape, jnp.float32)
        f32 = jnp.float32
        done = pl.pallas_call(
            functools.partial(kernel, (n_lon, n_lat, columns, height)),
            out_shape=(pltpu.VMEM(previous.shape, f32), pltpu.VMEM(previous.shape, f32)),
            in_specs=[pl.BlockSpec(memory_space=pl.ANY)] * 7,
            out_specs=[pl.BlockSpec(memory_space=pltpu.VMEM)] * 2,
            scratch_shapes=[
                pltpu.VMEM(sea_mask.shape, sea_mask.dtype),
                pltpu.VMEM((2, *previous.shape), f32),
                pltpu.VMEM((4, *east_speed.shape), f32),
                pltpu.VMEM((STEPS + 1, 2, 2, 2, tiles + 1, rows, LANES), f32),
                pltpu.VMEM((2, 4, tiles + 1, rows, LANES), f32),
                pltpu.VMEM((2, 8, columns, LANES), f32),
                pltpu.VMEM((2, 2, tiles + 1, rows, LANES), f32),
                pltpu.VMEM((2, 2, 2, tiles + 1, rows, LANES), f32),
                pltpu.VMEM((2, 2, columns, LANES), f32),
                pltpu.VMEM((2, 2, rows, LANES), f32),
                pltpu.SemaphoreType.DMA((7,)),
                pltpu.SemaphoreType.DMA((2, 2, 11)),
                pltpu.SemaphoreType.DMA((2, 2, 11)),
                pltpu.SemaphoreType.DMA((2, 2, 3)),
                pltpu.SemaphoreType.DMA((2, 2, 3)),
                pltpu.SemaphoreType.DMA((2, 2)),
            ],
            compiler_params=pltpu.CompilerParams(
                collective_id=0, has_side_effects=True, vmem_limit_bytes=60 * 2**20
            ),
            cost_estimate=pl.CostEstimate(
                flops=30 * STEPS * previous.size, bytes_accessed=16 * previous.size, transcendentals=0
            ),
        )(previous, current, east_speed, north_speed, east_mix, north_mix, sea_mask)
        def hand_over(a, b, x, y, sems):
            copies = [
                pltpu.make_async_copy(src.at[tr], dst.at[tr], sems.at[i, tr])
                for i, (src, dst) in enumerate(((a, x), (b, y)))
                for tr in range(2)
            ]
            for c in copies:
                c.start()
            for c in copies:
                c.wait()

        return pl.pallas_call(
            hand_over,
            out_shape=(field, field),
            in_specs=[pl.BlockSpec(memory_space=pl.ANY)] * 2,
            out_specs=[pl.BlockSpec(memory_space=pl.ANY)] * 2,
            scratch_shapes=[pltpu.SemaphoreType.DMA((2, 2))],
            name="hand_over",
            compiler_params=pltpu.CompilerParams(vmem_limit_bytes=2**20),
        )(*done)


    return jax.shard_map(
        shards,
        mesh=mesh,
        in_specs=(
            P(None, None, "lon", "lat"),
            P(None, None, "lon", "lat"),
            P(None, "lon", "lat"),
            P(None, "lon", "lat"),
            P(None, "lon", "lat"),
            P(None, "lon", "lat"),
            P("lon", "lat"),
        ),
        out_specs=(P(None, None, "lon", "lat"), P(None, None, "lon", "lat")),
        check_vma=False,
    )
```
